256 devices in a mesh: group: 8 (over z), leaf: 32 (over y, x, core).
Axes of the slice: x: 4, y: 4, z: 8, core: 2. Of those that a mesh axis runs over, the one named last changes fastest.
Arguments:
- observations: float32 [64, 262144], P(None, ('group', 'leaf')), may hold values from -6 to 6
- coordinates: float32 [3, 262144], P(None, ('group', 'leaf')), may hold values from 0 to 64, as said below
- proxies: float32 [256, 3, 64], P(('group', 'leaf')), may hold values from 0 to 64, as said below
- noise_variance: float32 [262144], P(('group', 'leaf')), may hold values from 0.5 to 2
- ordering: int32 [256, 1024], P(('group', 'leaf')), may hold values from 0 to 1023, each once within a row
- near_list: int32 [256, 7], P(('group', 'leaf')), may hold values from 0 to 255, as said below
- far_within: int32 [256, 6], P(('group', 'leaf')), may hold values from 0 to 31, as said below
- far_across: int32 [256, 7, 2], P(('group', 'leaf')), may hold values from 0 to 31, as said below
- couplings: bfloat16 [256, 20, 64, 64], P(('group', 'leaf')), may hold values from -0.3125 to 0.3125
Outputs:
- gain: float32 [64, 262144], P(None, ('group', 'leaf'))
- residual: float32 [64, 262144], P(None, ('group', 'leaf'))
The draws below stay inside these ranges and needn't reach their ends.
Inputs may be any that keep to these rules, and one draw needn't show every extreme that they name: `near_list`: row L names seven distinct leaves (L + d) mod 256 with d among -4, -3, -2, -1, 1, 2, 3, 4, in ascending order of d; the missing d is drawn for each leaf on its own and may be the same for different leaves. `far_within`: row L names 6 distinct leaves of L's own group by their index within the group, never L itself. `far_across`: entry [L, k, a] names, by its index within the group, a leaf of the group k + 1 places after L's own group, modulo the number of groups; the 2 entries of one [L, k] are distinct. Point coordinate 0 of leaf L lies in [L / 4, (L + 1) / 4]; coordinates 1 and 2 lie in [0, 8]. `proxies`: proxy coordinate 0 of leaf L lies in [L / 4, (L + 1) / 4]; coordinates 1 and 2 lie in [0, 8].
All inputs are finite; a program needn't handle non-finite values.
Results may differ from the reference program's by a relative error of at most 0.0045.
Values may be sent and summed in bfloat16 or wider, within the bound.
No kernel may reach another device: no remote copies, remote signals or barrier semaphores. Data moves between devices by JAX's collectives and lax.ppermute only.
A program may use at most 128 MiB of HBM per device.

```python
import math
import jax
import jax.numpy as jnp
from jax import lax

LEAF_PTS = 1024
COLS = 64
RANK = 64
FW = 6
ACROSS = 2
ITERS = 2
LEAVES = 256
POINTS = 262144
FAR = 20
N_GROUP = 8
N_LEAF = 32


slab_width = 0.25


side_length = 8.0


neighbour_offsets = (-4, -3, -2, -1, 1, 2, 3, 4)


def place_points(key, leaf_ids, count):
    uniform = jax.random.uniform(key, (3, count), jnp.float32)
    across = uniform[1:]
    first = (leaf_ids.astype(jnp.float32) + uniform[0]) * slab_width
    return jnp.concatenate([first[None, :], across * side_length], axis=0)


def draw_coordinates(key, part):
    leaf_ids = jnp.arange(POINTS, dtype=jnp.int32) // LEAF_PTS
    return place_points(jax.random.fold_in(key, 11), leaf_ids, POINTS)


def draw_proxies(key, part):
    leaf_ids = jnp.arange(LEAVES * RANK, dtype=jnp.int32) // RANK
    placed = place_points(jax.random.fold_in(key, 13), leaf_ids, LEAVES * RANK)
    return placed.reshape(3, LEAVES, RANK).transpose(1, 0, 2)


def draw_near_list(key, part):
    offsets = jnp.array(neighbour_offsets, jnp.int32)
    dropped = jax.random.randint(jax.random.fold_in(key, 17), (LEAVES,), 0, 8)
    columns = jnp.arange(7, dtype=jnp.int32)[None, :]
    chosen = columns + (columns >= dropped[:, None]).astype(jnp.int32)
    leaf_ids = jnp.arange(LEAVES, dtype=jnp.int32)[:, None]
    return ((leaf_ids + offsets[chosen]) % LEAVES).astype(jnp.int32)


def draw_far_within(key, part):
    candidates = jnp.arange(N_LEAF, dtype=jnp.int32)
    scores = jax.random.randint(jax.random.fold_in(key, 19), (LEAVES, N_LEAF), 0, 1 << 20) * N_LEAF + candidates[None, :]
    own_place = jnp.arange(LEAVES, dtype=jnp.int32) % N_LEAF
    scores = jnp.where(candidates[None, :] == own_place[:, None], 1 << 30, scores)
    return jnp.argsort(scores, axis=1)[:, :FW].astype(jnp.int32)


def draw_far_across(key, part):
    candidates = jnp.arange(N_LEAF, dtype=jnp.int32)
    scores = jax.random.randint(jax.random.fold_in(key, 23), (LEAVES, N_GROUP - 1, N_LEAF), 0, 1 << 20) * N_LEAF + candidates[None, None, :]
    return jnp.argsort(scores, axis=2)[:, :, :ACROSS].astype(jnp.int32)


def level_of(rng, dims, pieces, least, high):
    level, own = 1.0, jax.random.fold_in(rng, 6)
    for axis_at, shards_of in pieces:
        heights = jnp.exp(jax.random.uniform(jax.random.fold_in(own, axis_at), (shards_of,), jnp.float32, least / len(pieces), high / len(pieces)))
        level = level * jnp.repeat(heights, dims[axis_at] // shards_of).reshape([-1 if axis == axis_at else 1 for axis in range(len(dims))])
    return level


def noise(rng, extent, deviation, bound, shards=(), kind=jnp.bfloat16):
    values = jax.random.normal(rng, extent, jnp.float32) * deviation
    if len(shards) > 0:
        values = level_of(rng, extent, shards, -0.22, 0.18) * values
    return jnp.clip(values, min=-bound, max=bound).astype(kind)


def setup_inputs(seed: int = 0) -> dict:
    splits = jax.random.split(jax.random.key(seed), 10)
    return {
        "observations": noise(splits[0], (COLS, POINTS), 1.0, 6.0, ((1, 256),), jnp.float32),
        "coordinates": draw_coordinates(jax.random.fold_in(splits[9], 71), 0),
        "proxies": draw_proxies(jax.random.fold_in(splits[9], 71), 0),
        "noise_variance": jnp.clip(jnp.exp(math.log(2.0) - 1.3862944 * jax.random.uniform(splits[3], (POINTS,), jnp.float32) ** level_of(splits[3], (POINTS,), ((0, 256),), -0.2, 0.2)), 0.5, 2.0),
        "ordering": jax.vmap(lambda own: jax.random.permutation(own, LEAF_PTS))(jax.random.split(splits[4], LEAVES)).reshape((LEAVES, LEAF_PTS)).astype(jnp.int32),
        "near_list": draw_near_list(jax.random.fold_in(splits[9], 71), 0),
        "far_within": draw_far_within(jax.random.fold_in(splits[9], 71), 0),
        "far_across": draw_far_across(jax.random.fold_in(splits[9], 71), 0),
        "couplings": noise(splits[8], (LEAVES, FAR, RANK, RANK), (RANK * FAR // 4) ** -0.5, 0.3125, ((0, 256),)),
    }


length_scale = 0.5
kernel_scale = 8.0
lower_bound = 0.5
upper_bound = 4.0

def kernel_tile(source, target):
    squared = (source[0][:, None] - target[0][None, :]) ** 2
    squared = squared + (source[1][:, None] - target[1][None, :]) ** 2
    squared = squared + (source[2][:, None] - target[2][None, :]) ** 2
    return jnp.exp(-jnp.sqrt(squared) / length_scale)

def far_sources(far_within, far_across):
    leaf_ids = jnp.arange(LEAVES, dtype=jnp.int32)
    group_ids = leaf_ids // N_LEAF
    within = group_ids[:, None] * N_LEAF + far_within
    places = jnp.arange(1, N_GROUP, dtype=jnp.int32)
    others = (group_ids[:, None] + places[None, :]) % N_GROUP
    across = others[:, :, None] * N_LEAF + far_across
    return jnp.concatenate([within, across.reshape(LEAVES, -1)], axis=1).astype(jnp.int32)

def apply_operator(field, coords, leaf_basis, noise_leaf, tile_sources, far_ids, couplings):
    rounded = field.astype(jnp.bfloat16)
    packed = jnp.einsum('lcp,lrp->lcr', rounded.astype(jnp.float32), leaf_basis.astype(jnp.float32)).astype(jnp.bfloat16)

    def one_leaf(leaf_index):

        def add_tile(running, source_leaf):
            kernel_block = kernel_tile(coords[source_leaf], coords[leaf_index]).astype(jnp.bfloat16)
            return (running + jnp.dot(rounded[source_leaf], kernel_block, preferred_element_type=jnp.float32), None)
        near_part, _ = lax.scan(add_tile, jnp.zeros((COLS, LEAF_PTS), jnp.float32), tile_sources[leaf_index])
        listed = packed[far_ids[leaf_index]].astype(jnp.float32)
        spread = jnp.einsum('fcs,frs->cr', listed, couplings[leaf_index].astype(jnp.float32)).astype(jnp.bfloat16)
        far_part = jnp.dot(spread, leaf_basis[leaf_index], preferred_element_type=jnp.float32)
        return near_part + far_part
    kernel_part = lax.map(one_leaf, jnp.arange(LEAVES, dtype=jnp.int32))
    return noise_leaf * field + kernel_part / kernel_scale

def place_back(values, ordering):

    def one_leaf(block, point_order):
        return jnp.zeros_like(block).at[:, point_order].set(block)
    return jax.vmap(one_leaf)(values, ordering)

def reference(observations, coordinates, proxies, noise_variance, ordering, near_list, far_within, far_across, couplings):
    coords = coordinates.reshape(3, LEAVES, LEAF_PTS).transpose(1, 0, 2)
    sensor_values = observations.reshape(COLS, LEAVES, LEAF_PTS).transpose(1, 0, 2)
    right_side = jnp.take_along_axis(sensor_values, ordering[:, None, :], axis=2)
    noise_leaf = jnp.take_along_axis(noise_variance.reshape(LEAVES, LEAF_PTS), ordering, axis=1)[:, None, :]
    leaf_basis = jax.vmap(kernel_tile)(proxies, coords).astype(jnp.bfloat16)
    tile_sources = jnp.concatenate([jnp.arange(LEAVES, dtype=jnp.int32)[:, None], near_list], axis=1).astype(jnp.int32)
    far_ids = far_sources(far_within, far_across)
    centre = (upper_bound + lower_bound) / 2.0
    half_width = (upper_bound - lower_bound) / 2.0
    ratio_now = 1.0 / (centre / half_width)
    solution = jnp.zeros_like(right_side)
    residual_field = right_side
    direction = right_side / centre
    for iteration in range(ITERS):
        solution = solution + direction
        residual_field = residual_field - apply_operator(direction, coords, leaf_basis, noise_leaf, tile_sources, far_ids, couplings)
        if iteration + 1 < ITERS:
            ratio_next = 1.0 / (2.0 * centre / half_width - ratio_now)
            direction = ratio_next * ratio_now * direction + 2.0 * ratio_next / half_width * residual_field
            ratio_now = ratio_next
    gain = place_back(solution, ordering).transpose(1, 0, 2).reshape(COLS, POINTS)
    residual = place_back(residual_field, ordering).transpose(1, 0, 2).reshape(COLS, POINTS)
    return (gain, residual)
```

```python
import functools

import jax
import jax.numpy as jnp
from jax import lax
from jax.experimental import pallas as pl
from jax.experimental.pallas import tpu as pltpu
from jax.sharding import PartitionSpec as P

ITERS = 2
COLS = 64
POINTS = 1024
RANK = 64
CHUNK = 256
STEP = 16

length_scale = 0.5
kernel_scale = 8.0
lower_bound = 0.5
upper_bound = 4.0
centre = (upper_bound + lower_bound) / 2.0
half_width = (upper_bound - lower_bound) / 2.0
SCALE = 1.4426950408889634 / length_scale
ratio_first = 1.0 / (centre / half_width)
ratio_second = 1.0 / (2.0 * centre / half_width - ratio_first)
ALONG = ratio_second * ratio_first
ACROSS = 2.0 * ratio_second / half_width

F32, BF16 = jnp.float32, jnp.bfloat16
LAST = (((1,), (1,)), ((), ()))
VMEM = pl.BlockSpec(memory_space=pltpu.VMEM)
SMEM = pl.BlockSpec(memory_space=pltpu.SMEM)
BOTH = ("group", "leaf")


def shape(dims, kind):
    return jax.ShapeDtypeStruct(dims, kind)


def call(body, outs, ins, args, cost, scratch=(), aliases=None, name=None):
    several = isinstance(outs, (list, tuple))
    return pl.pallas_call(
        body,
        out_shape=outs,
        in_specs=ins,
        out_specs=[VMEM] * len(outs) if several else VMEM,
        scratch_shapes=list(scratch),
        input_output_aliases=aliases or {},
        compiler_params=pltpu.CompilerParams(vmem_limit_bytes=20 * 2**20),
        cost_estimate=pl.CostEstimate(
            flops=int(cost * 1e9), bytes_accessed=int(cost * 1e5), transcendentals=0
        ),
        name=name,
    )(*args)


def distance_kernel(squared):
    kept = jnp.maximum(squared, 1e-30)
    return jnp.exp2(-(kept * lax.rsqrt(kept)))


def coordinate_rows(tail):
    parts = tail.astype(F32)
    return parts[0:3] + parts[3:6] + parts[6:9]


def prepare_kernel(obs_ref, order_ref, coord_ref, message_ref, column_ref, onehot):
    message_ref[0:COLS, :] = (obs_ref[...] / centre).astype(BF16)
    scaled = coord_ref[...] * SCALE
    high = scaled.astype(BF16)
    left = scaled - high.astype(F32)
    middle = left.astype(BF16)
    low = (left - middle.astype(F32)).astype(BF16)
    parts = jnp.concatenate(
        [high.astype(F32), middle.astype(F32), low.astype(F32), jnp.zeros((119, POINTS), F32)],
        axis=0,
    ).astype(BF16)
    order = jnp.broadcast_to(order_ref[...], (STEP, POINTS))
    slot = lax.broadcasted_iota(jnp.int32, (STEP, POINTS), 0)
    for first in range(0, POINTS, CHUNK):
        for row in range(first, first + CHUNK, STEP):
            onehot[row : row + STEP, :] = jnp.where(order == slot + row, 1.0, 0.0).astype(BF16)
        placed = lax.dot_general(
            onehot[first : first + CHUNK, :], parts, LAST, preferred_element_type=F32
        )
        for c in range(3):
            value = placed[:, c : c + 1] + placed[:, 3 + c : 4 + c] + placed[:, 6 + c : 7 + c]
            column_ref[c, first : first + CHUNK, :] = jnp.broadcast_to(value, (CHUNK, 128))
        message_ref[COLS : COLS + 16, first : first + CHUNK] = placed.T[0:16, :].astype(BF16)


def half_of_chip(block):
    wide = jnp.concatenate([block, block], axis=1)
    lane = lax.broadcasted_iota(jnp.int32, (COLS, 2 * RANK), 1)
    core = lax.rem(lax.axis_index("leaf"), 2)
    return jnp.where(lane // RANK == core, wide, 0.0).astype(BF16)


def basis_kernel(message_ref, proxy_ref, basis_ref, packed_ref):
    rows = coordinate_rows(message_ref[COLS : COLS + 16, :])
    squared = None
    for c in range(3):
        apart = proxy_ref[:, c : c + 1] * SCALE - rows[c : c + 1, :]
        squared = apart * apart if squared is None else squared + apart * apart
    basis = distance_kernel(squared).astype(BF16)
    basis_ref[...] = basis
    packed_ref[...] = half_of_chip(
        lax.dot_general(message_ref[0:COLS, :], basis, LAST, preferred_element_type=F32)
    )


def build_and_apply(message_ref, column_ref, tile_ref, total_ref, first_block):
    coords = coordinate_rows(message_ref[COLS : COLS + 16, :])
    rows = [jnp.broadcast_to(coords[c : c + 1, :], (STEP, POINTS)) for c in range(3)]
    field = message_ref[0:COLS, :]
    for first in range(0, POINTS, CHUNK):
        for row in range(first, first + CHUNK, STEP):
            pieces = []
            for lane in range(0, POINTS, 128):
                squared = None
                for c in range(3):
                    apart = column_ref[c, row : row + STEP, :] - rows[c][:, lane : lane + 128]
                    squared = apart * apart if squared is None else squared + apart * apart
                pieces.append(distance_kernel(squared).astype(BF16))
            tile_ref[row : row + STEP, :] = jnp.concatenate(pieces, axis=1)
        product = lax.dot_general(
            tile_ref[first : first + CHUNK, :], field, LAST, preferred_element_type=F32
        )
        if first_block:
            total_ref[first : first + CHUNK, :] = product
        else:
            total_ref[first : first + CHUNK, :] += product


def own_tile_kernel(message_ref, column_ref, tile_ref, total_ref):
    build_and_apply(message_ref, column_ref, tile_ref, total_ref, True)


def near_tile_kernel(place, flag_ref, message_ref, column_ref, total_in, tile_ref, total_ref):
    @pl.when(flag_ref[place] != 0)
    def _():
        build_and_apply(message_ref, column_ref, tile_ref, total_ref, False)


def apply_own_kernel(field_ref, tile_ref, total_ref):
    total_ref[...] = lax.dot_general(tile_ref[...], field_ref[...], LAST, preferred_element_type=F32)


def apply_near_kernel(places, flag_ref, *refs):
    count = len(places)
    total_ref = refs[-1]
    for at, place in enumerate(places):

        @pl.when(flag_ref[place] != 0)
        def _(at=at):
            total_ref[...] += lax.dot_general(
                refs[count + at][...], refs[at][...], LAST, preferred_element_type=F32
            )


def select_kernel(*refs):
    gathered, wanted = refs[0:4], refs[4:11]
    within_ref, sends, inside_ref, held = refs[11], refs[12:19], refs[19], refs[20]
    for dx in range(4):
        held[4 * dx : 4 * dx + 4] = gathered[dx][...]
    mine = lax.axis_index("leaf")
    my_y, my_x = mine // 8, lax.rem(mine // 2, 4)
    low_half = lax.broadcasted_iota(jnp.int32, (COLS, 2 * RANK), 1) < RANK

    def pair(first, second):
        halves = []
        for leaf, half in ((first, 0), (second, 1)):
            y, x, core = leaf // 8, lax.rem(leaf // 2, 4), lax.rem(leaf, 2)
            at = lax.rem(x - my_x + 4, 4) * 4 + lax.rem(y - my_y + 4, 4)
            block = held[at].astype(F32)
            turned = jnp.concatenate([block[:, RANK:], block[:, :RANK]], axis=1)
            same = jnp.full((COLS, 2 * RANK), core, jnp.int32) == half
            halves.append(jnp.where(same, block, turned))
        return jnp.where(low_half, halves[0], halves[1]).astype(BF16)

    for k in range(7):
        sends[k][...] = pair(wanted[k][0, k, 0], wanted[k][0, k, 1])
    for k in range(3):
        inside_ref[k] = pair(within_ref[0, 2 * k], within_ref[0, 2 * k + 1])


def kernel_part(inside_ref, arrived, coupling_ref, basis_ref, total_ref):
    spread = None
    for k in range(10):
        source = inside_ref[k] if k < 3 else arrived[k - 3][...]
        term = lax.dot_general(source, coupling_ref[k], LAST, preferred_element_type=F32)
        spread = term if spread is None else spread + term
    far = jnp.dot(spread.astype(BF16), basis_ref[...], preferred_element_type=F32)
    return (total_ref[...].T + far) / kernel_scale


def update_kernel(*refs):
    obs_ref, noise_ref, inside_ref = refs[0:3]
    arrived, coupling_ref, basis_ref, total_ref = refs[3:10], refs[10], refs[11], refs[12]
    gain_ref, residual_ref, direction_ref, rounded_ref, packed_ref = refs[13:18]
    right_side = obs_ref[...]
    direction = right_side / centre
    applied = noise_ref[...] * direction + kernel_part(
        inside_ref, arrived, coupling_ref, basis_ref, total_ref
    )
    residual = right_side - applied
    later = ALONG * direction + ACROSS * residual
    gain_ref[...] = direction + later
    residual_ref[...] = residual
    direction_ref[...] = later
    rounded = later.astype(BF16)
    rounded_ref[...] = rounded
    packed_ref[...] = half_of_chip(
        lax.dot_general(rounded, basis_ref[...], LAST, preferred_element_type=F32)
    )


def finish_kernel(*refs):
    before_ref, direction_ref, noise_ref, inside_ref = refs[0:4]
    arrived, coupling_ref, basis_ref, total_ref = refs[4:11], refs[11], refs[12], refs[13]
    applied = noise_ref[...] * direction_ref[...] + kernel_part(
        inside_ref, arrived, coupling_ref, basis_ref, total_ref
    )
    refs[14][...] = before_ref[...] - applied


def from_ahead(value, axis, steps):
    count = lax.axis_size(axis)
    return lax.ppermute(value, axis, [(s, (s - steps) % count) for s in range(count)])


def from_chip_x(value, steps):
    pairs = []
    for s in range(32):
        row, x, core = s // 8, (s // 2) % 4, s % 2
        pairs.append((s, row * 8 + ((x - steps) % 4) * 2 + core))
    return lax.ppermute(value, "leaf", pairs)


def from_partner(value):
    return lax.ppermute(value, "leaf", [(s, s ^ 1) for s in range(32)])


def spread_near(block, core):
    partner = from_partner(block)
    ahead2, behind2 = from_ahead(block, BOTH, 2), from_ahead(block, BOTH, -2)
    ahead4, behind4 = from_ahead(block, BOTH, 4), from_ahead(block, BOTH, -4)
    partner2, partner_2 = from_partner(ahead2), from_partner(behind2)
    partner4 = from_partner(jnp.where(core == 0, ahead4, behind4))
    return [partner, ahead2, behind2, partner2, partner_2, ahead4, behind4, partner4]


def gather_group(packed):
    chip = packed + from_partner(packed)
    column = jnp.stack([chip] + [from_ahead(chip, "leaf", 8 * dy) for dy in (1, 2, 3)])
    return [column] + [from_chip_x(column, dx) for dx in (1, 2, 3)]


def far_blocks(packed, wanted, far_within):
    picked = call(
        select_kernel,
        [shape((COLS, 2 * RANK), BF16)] * 7 + [shape((3, COLS, 2 * RANK), BF16)],
        [VMEM] * 4 + [SMEM] * 8,
        (*gather_group(packed), *wanted, far_within),
        0.7,
        [pltpu.VMEM((16, COLS, 2 * RANK), BF16)],
        name="select",
    )
    arrived = [from_ahead(picked[k], "group", k + 1) for k in range(7)]
    return picked[7], arrived


def local(
    observations,
    coordinates,
    proxies,
    noise_variance,
    ordering,
    near_list,
    far_within,
    far_across,
    couplings,
):
    leaves = lax.axis_size(BOTH)
    leaf_id = lax.axis_index(BOTH)
    core = leaf_id % 2
    wanted = [from_ahead(far_across, "group", -(k + 1)) for k in range(7)]
    even = jnp.array([1, 2, -2, 3, -1, 4, -4, -3], jnp.int32)
    odd = jnp.array([-1, 2, -2, 1, -3, 4, -4, 3], jnp.int32)
    offsets = jnp.where(core == 0, even, odd)
    targets = (leaf_id + offsets + leaves) % leaves
    flags = jnp.any(near_list[0][None, :] == targets[:, None], axis=1).astype(jnp.int32)
    paired = couplings[0].reshape(10, 2, RANK, RANK).transpose(0, 2, 1, 3).reshape(10, RANK, 2 * RANK)
    noise = noise_variance[None, :]

    message, column = call(
        prepare_kernel,
        [shape((COLS + 16, POINTS), BF16), shape((3, POINTS, 128), F32)],
        [VMEM] * 3,
        (observations, ordering, coordinates),
        2.0,
        [pltpu.VMEM((POINTS, POINTS), BF16)],
        name="prepare",
    )
    messages = spread_near(message, core)
    basis, packed = call(
        basis_kernel,
        [shape((RANK, POINTS), BF16), shape((COLS, 2 * RANK), BF16)],
        [VMEM] * 2,
        (message, proxies[0].T),
        0.7,
        name="basis",
    )
    tile_shape, total_shape = shape((POINTS, POINTS), BF16), shape((POINTS, COLS), F32)
    own_tile, total = call(
        own_tile_kernel, [tile_shape, total_shape], [VMEM] * 2, (message, column), 2.0, name="own_tile"
    )
    tiles = []
    for place in range(8):
        tile, total = call(
            functools.partial(near_tile_kernel, place),
            [tile_shape, total_shape],
            [SMEM] + [VMEM] * 3,
            (flags, messages[place], column, total),
            2.0,
            aliases={3: 1},
            name="near_tile",
        )
        tiles.append(tile)
    inside, arrived = far_blocks(packed, wanted, far_within)
    field = shape((COLS, POINTS), F32)
    gain, residual, direction, rounded, packed = call(
        update_kernel,
        [field, field, field, shape((COLS, POINTS), BF16), shape((COLS, 2 * RANK), BF16)],
        [VMEM] * 13,
        (observations, noise, inside, *arrived, paired, basis, total),
        1.5,
        name="update",
    )
    blocks = spread_near(rounded, core)
    total = call(
        apply_own_kernel, total_shape, [VMEM] * 2, (rounded, own_tile), 0.7, name="apply_own"
    )
    for places in ((0,), (1, 2), (3, 4), (5, 6), (7,)):
        total = call(
            functools.partial(apply_near_kernel, places),
            total_shape,
            [SMEM] + [VMEM] * (2 * len(places) + 1),
            (flags, *(blocks[p] for p in places), *(tiles[p] for p in places), total),
            0.7 * len(places),
            aliases={2 * len(places) + 1: 0},
            name="apply_near",
        )
    inside, arrived = far_blocks(packed, wanted, far_within)
    residual = call(
        finish_kernel,
        field,
        [VMEM] * 14,
        (residual, direction, noise, inside, *arrived, paired, basis, total),
        1.0,
        name="finish",
    )
    return (gain, residual)


def solution(mesh):
    placed = (
        P(None, ("group", "leaf")),
        P(None, ("group", "leaf")),
        P(("group", "leaf"), None, None),
        P(("group", "leaf")),
        P(("group", "leaf"), None),
        P(("group", "leaf"), None),
        P(("group", "leaf"), None),
        P(("group", "leaf"), None, None),
        P(("group", "leaf"), None, None, None),
    )
    return jax.shard_map(
        local,
        mesh=mesh,
        in_specs=placed,
        out_specs=(P(None, ("group", "leaf")), P(None, ("group", "leaf"))),
        check_vma=False,
    )
```

```python
import functools

import jax
import jax.numpy as jnp
from jax import lax
from jax.experimental import pallas as pl
from jax.experimental.pallas import tpu as pltpu
from jax.sharding import PartitionSpec as P

ITERS = 2
COLS = 64
POINTS = 1024
RANK = 64
CHUNK = 256
STEP = 16

length_scale = 0.5
kernel_scale = 8.0
lower_bound = 0.5
upper_bound = 4.0
centre = (upper_bound + lower_bound) / 2.0
half_width = (upper_bound - lower_bound) / 2.0
SCALE = 1.4426950408889634 / length_scale
ratio_first = 1.0 / (centre / half_width)
ratio_second = 1.0 / (2.0 * centre / half_width - ratio_first)
ALONG = ratio_second * ratio_first
ACROSS = 2.0 * ratio_second / half_width

F32, BF16 = jnp.float32, jnp.bfloat16
LAST = (((1,), (1,)), ((), ()))
VMEM = pl.BlockSpec(memory_space=pltpu.VMEM)
SMEM = pl.BlockSpec(memory_space=pltpu.SMEM)
BOTH = ("group", "leaf")


def shape(dims, kind):
    return jax.ShapeDtypeStruct(dims, kind)


def call(body, outs, ins, args, cost, scratch=(), aliases=None, name=None):
    several = isinstance(outs, (list, tuple))
    return pl.pallas_call(
        body,
        out_shape=outs,
        in_specs=ins,
        out_specs=[VMEM] * len(outs) if several else VMEM,
        scratch_shapes=list(scratch),
        input_output_aliases=aliases or {},
        compiler_params=pltpu.CompilerParams(vmem_limit_bytes=20 * 2**20),
        cost_estimate=pl.CostEstimate(
            flops=int(cost * 1e9), bytes_accessed=int(cost * 1e5), transcendentals=0
        ),
        name=name,
    )(*args)


def distance_kernel(squared):
    kept = jnp.maximum(squared, 1e-30)
    return jnp.exp2(-(kept * lax.rsqrt(kept)))


def coordinate_rows(tail):
    parts = tail.astype(F32)
    return parts[0:3] + parts[3:6] + parts[6:9]


def prepare_kernel(obs_hbm, order_hbm, coord_hbm, message_ref, column_ref, onehot, obs_ref, order_ref, coord_ref, sems):
    loads = [
        pltpu.make_async_copy(order_hbm, order_ref, sems.at[0]),
        pltpu.make_async_copy(coord_hbm, coord_ref, sems.at[1]),
        pltpu.make_async_copy(obs_hbm, obs_ref, sems.at[2]),
    ]
    for load in loads:
        load.start()
    loads[0].wait()
    loads[1].wait()
    scaled = coord_ref[...] * SCALE
    high = scaled.astype(BF16)
    left = scaled - high.astype(F32)
    middle = left.astype(BF16)
    low = (left - middle.astype(F32)).astype(BF16)
    parts = jnp.concatenate(
        [high.astype(F32), middle.astype(F32), low.astype(F32), jnp.zeros((119, POINTS), F32)],
        axis=0,
    ).astype(BF16)
    order = jnp.broadcast_to(order_ref[...], (STEP, POINTS))
    slot = lax.broadcasted_iota(jnp.int32, (STEP, POINTS), 0)
    for first in range(0, POINTS, CHUNK):
        for row in range(first, first + CHUNK, STEP):
            onehot[row : row + STEP, :] = jnp.where(order == slot + row, 1.0, 0.0).astype(BF16)
        placed = lax.dot_general(
            onehot[first : first + CHUNK, :], parts, LAST, preferred_element_type=F32
        )
        for c in range(3):
            value = placed[:, c : c + 1] + placed[:, 3 + c : 4 + c] + placed[:, 6 + c : 7 + c]
            column_ref[c, first : first + CHUNK, :] = jnp.broadcast_to(value, (CHUNK, 128))
        message_ref[COLS : COLS + 16, first : first + CHUNK] = placed.T[0:16, :].astype(BF16)
    loads[2].wait()
    message_ref[0:COLS, :] = (obs_ref[...] / centre).astype(BF16)


def half_of_chip(block):
    wide = jnp.concatenate([block, block], axis=1)
    lane = lax.broadcasted_iota(jnp.int32, (COLS, 2 * RANK), 1)
    core = lax.rem(lax.axis_index("leaf"), 2)
    return jnp.where(lane // RANK == core, wide, 0.0).astype(BF16)


def basis_kernel(message_ref, proxy_ref, basis_ref, wide_ref):
    rows = coordinate_rows(message_ref[COLS : COLS + 16, :])
    squared = None
    for c in range(3):
        apart = proxy_ref[:, c : c + 1] * SCALE - rows[c : c + 1, :]
        squared = apart * apart if squared is None else squared + apart * apart
    basis = distance_kernel(squared).astype(BF16)
    basis_ref[...] = basis
    wide_ref[:, 0:POINTS] = message_ref[...]
    wide_ref[0:COLS, POINTS:] = half_of_chip(
        lax.dot_general(message_ref[0:COLS, :], basis, LAST, preferred_element_type=F32)
    )
    wide_ref[COLS : COLS + 16, POINTS:] = jnp.zeros((16, 2 * RANK), BF16)


def build_and_apply(block, column_ref, tile_ref, total_ref, first_block):
    coords = coordinate_rows(block[COLS : COLS + 16, 0:POINTS])
    rows = [jnp.broadcast_to(coords[c : c + 1, :], (STEP, POINTS)) for c in range(3)]
    field = block[0:COLS, 0:POINTS]
    for first in range(0, POINTS, CHUNK):
        for row in range(first, first + CHUNK, STEP):
            pieces = []
            for lane in range(0, POINTS, 128):
                squared = None
                for c in range(3):
                    apart = column_ref[c, row : row + STEP, :] - rows[c][:, lane : lane + 128]
                    squared = apart * apart if squared is None else squared + apart * apart
                pieces.append(distance_kernel(squared).astype(BF16))
            tile_ref[row : row + STEP, :] = jnp.concatenate(pieces, axis=1)
        product = lax.dot_general(
            tile_ref[first : first + CHUNK, :], field, LAST, preferred_element_type=F32
        )
        if first_block:
            total_ref[first : first + CHUNK, :] = product
        else:
            total_ref[first : first + CHUNK, :] += product


def chip_tiles_kernel(flag_ref, own_ref, partner_ref, column_ref, own_tile, partner_tile, total_ref):
    build_and_apply(own_ref, column_ref, own_tile, total_ref, True)

    @pl.when(flag_ref[0] != 0)
    def _():
        build_and_apply(partner_ref, column_ref, partner_tile, total_ref, False)


def pair_tiles_kernel(place, flag_ref, pair_ref, column_ref, total_in, tiles_ref, total_ref):
    total_ref[...] = total_in[...]

    @pl.loop(0, 2)
    def _(at):
        @pl.when(flag_ref[place + at] != 0)
        def _():
            build_and_apply(pair_ref.at[at], column_ref, tiles_ref.at[at], total_ref, False)


def apply_own_kernel(wide_ref, tile_ref, total_ref):
    total_ref[...] = lax.dot_general(
        tile_ref[...], wide_ref[:, 0:POINTS], LAST, preferred_element_type=F32
    )


def apply_near_kernel(places, flag_ref, *refs):
    count = len(places)
    total_ref = refs[-1]
    total_ref[...] = refs[-2][...]
    for which, (place, blocks) in enumerate(places):
        for at in range(blocks):

            @pl.when(flag_ref[place + at] != 0)
            def _(which=which, at=at, blocks=blocks):
                block, tile = refs[which], refs[count + which]
                if blocks == 2:
                    block, tile = block.at[at], tile.at[at]
                total_ref[...] += lax.dot_general(
                    tile[...], block[0:COLS, 0:POINTS], LAST, preferred_element_type=F32
                )


def select_kernel(*refs):
    gathered, wanted, within_ref = refs[0:4], refs[4], refs[5]
    sends, inside_ref, held = refs[6:10], refs[10], refs[11]
    for dx in range(4):
        held[4 * dx : 4 * dx + 4] = gathered[dx][...]
    mine, group = lax.axis_index("leaf"), lax.axis_index("group")
    my_y, my_x, my_core = mine // 8, lax.rem(mine // 2, 4), lax.rem(mine, 2)
    low_half = lax.broadcasted_iota(jnp.int32, (COLS, 2 * RANK), 1) < RANK

    def pair(first, second):
        halves = []
        for leaf, half in ((first, 0), (second, 1)):
            y, x, core = leaf // 8, lax.rem(leaf // 2, 4), lax.rem(leaf, 2)
            at = lax.rem(x - my_x + 4, 4) * 4 + lax.rem(y - my_y + 4, 4)
            block = held[at].astype(F32)
            turned = jnp.concatenate([block[:, RANK:], block[:, :RANK]], axis=1)
            same = jnp.full((COLS, 2 * RANK), core, jnp.int32) == half
            halves.append(jnp.where(same, block, turned))
        return jnp.where(low_half, halves[0], halves[1]).astype(BF16)

    for j in (1, 2, 3, 4):
        asker = lax.rem(jnp.where(my_core == 0, group + 8 - j, group + j), 8)
        k = jnp.where(my_core == 0, j - 1, 7 - j)
        for who in range(1 if j == 4 else 2):
            at = ((asker ^ group) * 2 + who) * 14 + k * 2
            sends[j - 1][who] = pair(wanted[at], wanted[at + 1])
    for k in range(3):
        inside_ref[k] = pair(within_ref[0, 2 * k], within_ref[0, 2 * k + 1])


def kernel_part(inside_ref, arrived, passed_ref, coupling_ref, basis_ref, total_ref):
    core = lax.rem(lax.axis_index("leaf"), 2)
    spread = None

    def add(spread, source, first):
        for a in range(2):
            half = source.astype(F32)[:, a * RANK : a * RANK + RANK].astype(BF16)
            term = lax.dot_general(half, coupling_ref[0, first + a], LAST, preferred_element_type=F32)
            spread = term if spread is None else spread + term
        return spread

    for k in range(3):
        spread = add(spread, inside_ref[k], 2 * k)
    for j in (1, 2, 3):
        near, away = 6 + 2 * (j - 1), 6 + 2 * (7 - j)
        spread = add(spread, arrived[j - 1][0], jnp.where(core == 0, near, away))
        spread = add(spread, passed_ref[j - 1], jnp.where(core == 0, away, near))
    spread = add(spread, arrived[3][0], 6 + 2 * 3)
    far = jnp.dot(spread.astype(BF16), basis_ref[...], preferred_element_type=F32)
    return (total_ref[...].T + far) / kernel_scale


def update_kernel(*refs):
    obs_ref, noise_ref, inside_ref, arrived, passed_ref = refs[0], refs[1], refs[2], refs[3:7], refs[7]
    coupling_ref, basis_ref, total_ref = refs[8:11]
    gain_ref, residual_ref, direction_ref, wide_ref = refs[11:15]
    right_side = obs_ref[...]
    direction = right_side / centre
    applied = noise_ref[...] * direction + kernel_part(
        inside_ref, arrived, passed_ref, coupling_ref, basis_ref, total_ref
    )
    residual = right_side - applied
    later = ALONG * direction + ACROSS * residual
    rounded = later.astype(BF16)
    wide_ref[:, 0:POINTS] = rounded
    wide_ref[:, POINTS:] = half_of_chip(
        lax.dot_general(rounded, basis_ref[...], LAST, preferred_element_type=F32)
    )
    gain_ref[...] = direction + later
    residual_ref[...] = residual
    direction_ref[...] = later


def finish_kernel(*refs):
    before_ref, direction_ref, noise_ref, inside_ref, arrived, passed_ref = (*refs[0:4], refs[4:8], refs[8])
    coupling_ref, basis_ref, total_ref = refs[9:12]
    applied = noise_ref[...] * direction_ref[...] + kernel_part(
        inside_ref, arrived, passed_ref, coupling_ref, basis_ref, total_ref
    )
    refs[12][...] = before_ref[...] - applied


def from_ahead(value, axis, steps):
    count = lax.axis_size(axis)
    return lax.ppermute(value, axis, [(s, (s - steps) % count) for s in range(count)])


def from_chip_x(value, steps):
    pairs = []
    for s in range(32):
        row, x, core = s // 8, (s // 2) % 4, s % 2
        pairs.append((s, row * 8 + ((x - steps) % 4) * 2 + core))
    return lax.ppermute(value, "leaf", pairs)


def from_both_sides(value, axis, chips, per_chip):
    count = lax.axis_size(axis)
    pairs = []
    for s in range(count):
        steps = -chips * per_chip if s % 2 == 0 else chips * per_chip
        pairs.append((s, (s + steps) % count))
    return lax.ppermute(value, axis, pairs)


def from_partner(value):
    return lax.ppermute(value, "leaf", [(s, s ^ 1) for s in range(32)])


def spread_near(wide, partner):
    pair = jnp.stack([wide[:, :POINTS], partner[:, :POINTS]])
    first = from_both_sides(pair, BOTH, 1, 2)
    second = from_both_sides(pair, BOTH, 2, 2)
    return first, from_partner(first), second, from_partner(second)


def gather_group(chip):
    column = jnp.stack([chip] + [from_ahead(chip, "leaf", 8 * dy) for dy in (1, 2, 3)])
    return [column] + [from_chip_x(column, dx) for dx in (1, 2, 3)]


def far_blocks(wide, partner, wanted, far_within):
    chip = wide[:COLS, POINTS:] + partner[:COLS, POINTS:]
    one, two = shape((1, COLS, 2 * RANK), BF16), shape((2, COLS, 2 * RANK), BF16)
    *sends, inside = call(
        select_kernel,
        [two, two, two, one, shape((3, COLS, 2 * RANK), BF16)],
        [VMEM] * 4 + [SMEM] * 2,
        (*gather_group(chip), wanted, far_within),
        0.7,
        [pltpu.VMEM((16, COLS, 2 * RANK), BF16)],
        name="select",
    )
    arrived = [from_both_sides(sends[j - 1], BOTH, j, 32) for j in (1, 2, 3, 4)]
    passed = from_partner(jnp.stack([arrived[j][1] for j in range(3)]))
    return (inside, *arrived, passed)


def local(
    observations,
    coordinates,
    proxies,
    noise_variance,
    ordering,
    near_list,
    far_within,
    far_across,
    couplings,
):
    leaves = lax.axis_size(BOTH)
    leaf_id = lax.axis_index(BOTH)
    core = leaf_id % 2
    asked = jnp.stack([far_across[0], from_partner(far_across[0])]).reshape(28)
    wanted = asked[None]
    for bit in (1, 2, 4):
        other = lax.ppermute(wanted, "group", [(s, s ^ bit) for s in range(8)])
        wanted = jnp.concatenate([wanted, other])
    wanted = wanted.reshape(8 * 28)
    offsets = jnp.array([1, 2, 3, -1, -2, 4, 5, -3, -4], jnp.int32) * (1 - 2 * core)
    targets = (leaf_id + offsets + leaves) % leaves
    flags = jnp.any(near_list[0][None, :] == targets[:, None], axis=1).astype(jnp.int32)
    noise = noise_variance[None, :]

    message, column = call(
        prepare_kernel,
        [shape((COLS + 16, POINTS), BF16), shape((3, POINTS, 128), F32)],
        [pl.BlockSpec(memory_space=pltpu.HBM)] * 3,
        (observations, ordering, coordinates),
        2.0,
        [
            pltpu.VMEM((POINTS, POINTS), BF16),
            pltpu.VMEM((COLS, POINTS), F32),
            pltpu.VMEM((1, POINTS), jnp.int32),
            pltpu.VMEM((3, POINTS), F32),
            pltpu.SemaphoreType.DMA((3,)),
        ],
        name="prepare",
    )
    basis, wide = call(
        basis_kernel,
        [shape((RANK, POINTS), BF16), shape((COLS + 16, POINTS + 2 * RANK), BF16)],
        [VMEM] * 2,
        (message, proxies[0].T),
        0.7,
        name="basis",
    )
    partner = from_partner(wide)
    pairs = spread_near(wide, partner)
    tile_shape, total_shape = shape((POINTS, POINTS), BF16), shape((POINTS, COLS), F32)
    own_tile, partner_tile, total = call(
        chip_tiles_kernel,
        [tile_shape, tile_shape, total_shape],
        [SMEM] + [VMEM] * 3,
        (flags, wide, partner, column),
        4.0,
        name="chip_tiles",
    )
    tiles = []
    for at in range(4):
        tile, total = call(
            functools.partial(pair_tiles_kernel, 1 + 2 * at),
            [shape((2, POINTS, POINTS), BF16), total_shape],
            [SMEM] + [VMEM] * 3,
            (flags, pairs[at], column, total),
            4.0,
            name="pair_tiles",
        )
        tiles.append(tile)
    far = far_blocks(wide, partner, wanted, far_within)
    field = shape((COLS, POINTS), F32)
    gain, residual, direction, wide = call(
        update_kernel,
        [field, field, field, shape((COLS, POINTS + 2 * RANK), BF16)],
        [VMEM] * 11,
        (observations, noise, *far, couplings, basis, total),
        1.5,
        name="update",
    )
    partner = from_partner(wide)
    pairs = spread_near(wide, partner)
    total = call(
        apply_own_kernel, total_shape, [VMEM] * 2, (wide, own_tile), 0.7, name="apply_own"
    )
    for places in (((0, 1), (1, 2)), ((3, 2), (5, 2)), ((7, 2),)):
        blocks = [partner if p == 0 else pairs[p // 2] for p, _ in places]
        matching = [partner_tile if p == 0 else tiles[p // 2] for p, _ in places]
        total = call(
            functools.partial(apply_near_kernel, places),
            total_shape,
            [SMEM] + [VMEM] * (2 * len(places) + 1),
            (flags, *blocks, *matching, total),
            0.7 * sum(n for _, n in places),
            name="apply_near",
        )
    far = far_blocks(wide, partner, wanted, far_within)
    residual = call(
        finish_kernel,
        field,
        [VMEM] * 12,
        (residual, direction, noise, *far, couplings, basis, total),
        1.0,
        name="finish",
    )
    return (gain, residual)


def solution(mesh):
    placed = (
        P(None, ("group", "leaf")),
        P(None, ("group", "leaf")),
        P(("group", "leaf"), None, None),
        P(("group", "leaf")),
        P(("group", "leaf"), None),
        P(("group", "leaf"), None),
        P(("group", "leaf"), None),
        P(("group", "leaf"), None, None),
        P(("group", "leaf"), None, None, None),
    )
    return jax.shard_map(
        local,
        mesh=mesh,
        in_specs=placed,
        out_specs=(P(None, ("group", "leaf")), P(None, ("group", "leaf"))),
        check_vma=False,
    )
```

```python
import functools

import jax
import jax.numpy as jnp
from jax import lax
from jax.experimental import pallas as pl
from jax.experimental.pallas import tpu as pltpu
from jax.sharding import PartitionSpec as P

ITERS = 2
COLS = 64
POINTS = 1024
RANK = 64
CHUNK = 256
STEP = 16

length_scale = 0.5
kernel_scale = 8.0
lower_bound = 0.5
upper_bound = 4.0
centre = (upper_bound + lower_bound) / 2.0
half_width = (upper_bound - lower_bound) / 2.0
SCALE = 1.4426950408889634 / length_scale
ratio_first = 1.0 / (centre / half_width)
ratio_second = 1.0 / (2.0 * centre / half_width - ratio_first)
ALONG = ratio_second * ratio_first
ACROSS = 2.0 * ratio_second / half_width

F32, BF16 = jnp.float32, jnp.bfloat16
LAST = (((1,), (1,)), ((), ()))
VMEM = pl.BlockSpec(memory_space=pltpu.VMEM)
SMEM = pl.BlockSpec(memory_space=pltpu.SMEM)
BOTH = ("group", "leaf")


def shape(dims, kind):
    return jax.ShapeDtypeStruct(dims, kind)


def call(body, outs, ins, args, cost, scratch=(), aliases=None, name=None):
    several = isinstance(outs, (list, tuple))
    return pl.pallas_call(
        body,
        out_shape=outs,
        in_specs=ins,
        out_specs=[VMEM] * len(outs) if several else VMEM,
        scratch_shapes=list(scratch),
        input_output_aliases=aliases or {},
        compiler_params=pltpu.CompilerParams(vmem_limit_bytes=20 * 2**20),
        cost_estimate=pl.CostEstimate(
            flops=int(cost * 1e9), bytes_accessed=int(cost * 1e5), transcendentals=0
        ),
        name=name,
    )(*args)


def distance_kernel(squared):
    kept = jnp.maximum(squared, 1e-30)
    return jnp.exp2(-(kept * lax.rsqrt(kept)))


def coordinate_rows(tail):
    parts = tail.astype(F32)
    return parts[0:3] + parts[3:6] + parts[6:9]


def prepare_kernel(obs_hbm, order_hbm, coord_hbm, message_ref, column_ref, onehot, obs_ref, order_ref, coord_ref, sems):
    loads = [
        pltpu.make_async_copy(order_hbm, order_ref, sems.at[0]),
        pltpu.make_async_copy(coord_hbm, coord_ref, sems.at[1]),
        pltpu.make_async_copy(obs_hbm, obs_ref, sems.at[2]),
    ]
    for load in loads:
        load.start()
    loads[0].wait()
    loads[1].wait()
    scaled = coord_ref[...] * SCALE
    high = scaled.astype(BF16)
    left = scaled - high.astype(F32)
    middle = left.astype(BF16)
    low = (left - middle.astype(F32)).astype(BF16)
    parts = jnp.concatenate(
        [high.astype(F32), middle.astype(F32), low.astype(F32), jnp.zeros((119, POINTS), F32)],
        axis=0,
    ).astype(BF16)
    order = jnp.broadcast_to(order_ref[...], (STEP, POINTS))
    slot = lax.broadcasted_iota(jnp.int32, (STEP, POINTS), 0)
    for first in range(0, POINTS, CHUNK):
        for row in range(first, first + CHUNK, STEP):
            onehot[row : row + STEP, :] = jnp.where(order == slot + row, 1.0, 0.0).astype(BF16)
        placed = lax.dot_general(
            onehot[first : first + CHUNK, :], parts, LAST, preferred_element_type=F32
        )
        for c in range(3):
            value = placed[:, c : c + 1] + placed[:, 3 + c : 4 + c] + placed[:, 6 + c : 7 + c]
            column_ref[c, first : first + CHUNK, :] = jnp.broadcast_to(value, (CHUNK, 128))
        message_ref[COLS : COLS + 16, first : first + CHUNK] = placed.T[0:16, :].astype(BF16)
    loads[2].wait()
    message_ref[0:COLS, :] = (obs_ref[...] / centre).astype(BF16)


def half_of_chip(block):
    wide = jnp.concatenate([block, block], axis=1)
    lane = lax.broadcasted_iota(jnp.int32, (COLS, 2 * RANK), 1)
    core = lax.rem(lax.axis_index("leaf"), 2)
    return jnp.where(lane // RANK == core, wide, 0.0).astype(BF16)


def basis_kernel(message_ref, proxy_ref, basis_ref, wide_ref):
    rows = coordinate_rows(message_ref[COLS : COLS + 16, :])
    squared = None
    for c in range(3):
        apart = proxy_ref[:, c : c + 1] * SCALE - rows[c : c + 1, :]
        squared = apart * apart if squared is None else squared + apart * apart
    basis = distance_kernel(squared).astype(BF16)
    basis_ref[...] = basis
    wide_ref[:, 0:POINTS] = message_ref[...]
    wide_ref[0:COLS, POINTS:] = half_of_chip(
        lax.dot_general(message_ref[0:COLS, :], basis, LAST, preferred_element_type=F32)
    )
    wide_ref[COLS : COLS + 16, POINTS:] = jnp.zeros((16, 2 * RANK), BF16)


def build_and_apply(block, column_ref, tile_ref, total_ref, first_block):
    coords = coordinate_rows(block[COLS : COLS + 16, 0:POINTS])
    rows = [jnp.broadcast_to(coords[c : c + 1, :], (STEP, POINTS)) for c in range(3)]
    field = block[0:COLS, 0:POINTS]
    for first in range(0, POINTS, CHUNK):
        for row in range(first, first + CHUNK, STEP):
            pieces = []
            for lane in range(0, POINTS, 128):
                squared = None
                for c in range(3):
                    apart = column_ref[c, row : row + STEP, :] - rows[c][:, lane : lane + 128]
                    squared = apart * apart if squared is None else squared + apart * apart
                pieces.append(distance_kernel(squared).astype(BF16))
            tile_ref[row : row + STEP, :] = jnp.concatenate(pieces, axis=1)
        product = lax.dot_general(
            tile_ref[first : first + CHUNK, :], field, LAST, preferred_element_type=F32
        )
        if first_block:
            total_ref[first : first + CHUNK, :] = product
        else:
            total_ref[first : first + CHUNK, :] += product


def own_tile_kernel(own_ref, column_ref, own_tile, total_ref):
    build_and_apply(own_ref, column_ref, own_tile, total_ref, True)


def partner_tile_kernel(flag_ref, partner_ref, column_ref, total_in, tile_ref, total_ref):
    total_ref[...] = total_in[...]

    @pl.when(flag_ref[0] != 0)
    def _():
        build_and_apply(partner_ref, column_ref, tile_ref, total_ref, False)


def pair_tiles_kernel(place, flag_ref, pair_ref, column_ref, total_in, tiles_ref, total_ref):
    total_ref[...] = total_in[...]

    @pl.loop(0, 2)
    def _(at):
        @pl.when(flag_ref[place + at] != 0)
        def _():
            build_and_apply(pair_ref.at[at], column_ref, tiles_ref.at[at], total_ref, False)


def apply_own_kernel(wide_ref, tile_ref, total_ref):
    total_ref[...] = lax.dot_general(
        tile_ref[...], wide_ref[:, 0:POINTS], LAST, preferred_element_type=F32
    )


def apply_near_kernel(places, flag_ref, *refs):
    count = len(places)
    total_ref = refs[-1]
    total_ref[...] = refs[-2][...]
    for which, (place, blocks) in enumerate(places):
        for at in range(blocks):

            @pl.when(flag_ref[place + at] != 0)
            def _(which=which, at=at, blocks=blocks):
                block, tile = refs[which], refs[count + which]
                if blocks == 2:
                    block, tile = block.at[at], tile.at[at]
                total_ref[...] += lax.dot_general(
                    tile[...], block[0:COLS, 0:POINTS], LAST, preferred_element_type=F32
                )


def select_kernel(*refs):
    gathered, wanted, within_ref = refs[0:2], refs[2], refs[3]
    sends, inside_ref, held = refs[4:8], refs[8], refs[9]
    held[0:8] = gathered[0][...]
    held[8:16] = gathered[1][...]
    mine, group = lax.axis_index("leaf"), lax.axis_index("group")
    my_y, my_x, my_core = mine // 8, lax.rem(mine // 2, 4), lax.rem(mine, 2)
    low_half = lax.broadcasted_iota(jnp.int32, (COLS, 2 * RANK), 1) < RANK

    def pair(first, second):
        halves = []
        for leaf, half in ((first, 0), (second, 1)):
            y, x, core = leaf // 8, lax.rem(leaf // 2, 4), lax.rem(leaf, 2)
            at = (x ^ my_x) * 4 + (y ^ my_y)
            block = held[at].astype(F32)
            turned = jnp.concatenate([block[:, RANK:], block[:, :RANK]], axis=1)
            same = jnp.full((COLS, 2 * RANK), core, jnp.int32) == half
            halves.append(jnp.where(same, block, turned))
        return jnp.where(low_half, halves[0], halves[1]).astype(BF16)

    for j in (1, 2, 3, 4):
        asker = lax.rem(jnp.where(my_core == 0, group + 8 - j, group + j), 8)
        k = jnp.where(my_core == 0, j - 1, 7 - j)
        for who in range(1 if j == 4 else 2):
            at = ((asker ^ group) * 2 + who) * 14 + k * 2
            sends[j - 1][who] = pair(wanted[at], wanted[at + 1])
    for k in range(3):
        inside_ref[k] = pair(within_ref[0, 2 * k], within_ref[0, 2 * k + 1])


def kernel_part(inside_ref, arrived, passed_ref, coupling_ref, basis_ref, total_ref):
    core = lax.rem(lax.axis_index("leaf"), 2)
    spread = None

    def add(spread, source, first):
        for a in range(2):
            half = source.astype(F32)[:, a * RANK : a * RANK + RANK].astype(BF16)
            term = lax.dot_general(half, coupling_ref[0, first + a], LAST, preferred_element_type=F32)
            spread = term if spread is None else spread + term
        return spread

    for k in range(3):
        spread = add(spread, inside_ref[k], 2 * k)
    for j in (1, 2, 3):
        near, away = 6 + 2 * (j - 1), 6 + 2 * (7 - j)
        spread = add(spread, arrived[j - 1][0], jnp.where(core == 0, near, away))
        spread = add(spread, passed_ref[j - 1], jnp.where(core == 0, away, near))
    spread = add(spread, arrived[3][0], 6 + 2 * 3)
    far = jnp.dot(spread.astype(BF16), basis_ref[...], preferred_element_type=F32)
    return (total_ref[...].T + far) / kernel_scale


def update_kernel(*refs):
    obs_ref, noise_ref, inside_ref, arrived, passed_ref = refs[0], refs[1], refs[2], refs[3:7], refs[7]
    coupling_ref, basis_ref, total_ref = refs[8:11]
    gain_ref, residual_ref, direction_ref, wide_ref = refs[11:15]
    right_side = obs_ref[...]
    direction = right_side / centre
    applied = noise_ref[...] * direction + kernel_part(
        inside_ref, arrived, passed_ref, coupling_ref, basis_ref, total_ref
    )
    residual = right_side - applied
    later = ALONG * direction + ACROSS * residual
    rounded = later.astype(BF16)
    wide_ref[:, 0:POINTS] = rounded
    wide_ref[:, POINTS:] = half_of_chip(
        lax.dot_general(rounded, basis_ref[...], LAST, preferred_element_type=F32)
    )
    gain_ref[...] = direction + later
    residual_ref[...] = residual
    direction_ref[...] = later


def finish_kernel(*refs):
    before_ref, direction_ref, noise_ref, inside_ref, arrived, passed_ref = (*refs[0:4], refs[4:8], refs[8])
    coupling_ref, basis_ref, total_ref = refs[9:12]
    applied = noise_ref[...] * direction_ref[...] + kernel_part(
        inside_ref, arrived, passed_ref, coupling_ref, basis_ref, total_ref
    )
    refs[12][...] = before_ref[...] - applied


def from_ahead(value, axis, steps):
    count = lax.axis_size(axis)
    return lax.ppermute(value, axis, [(s, (s - steps) % count) for s in range(count)])


def exchange(value, axis, distance):
    count = lax.axis_size(axis)
    return lax.ppermute(value, axis, [(s, s ^ distance) for s in range(count)])


def from_both_sides(value, axis, chips, per_chip):
    count = lax.axis_size(axis)
    pairs = []
    for s in range(count):
        steps = -chips * per_chip if s % 2 == 0 else chips * per_chip
        pairs.append((s, (s + steps) % count))
    return lax.ppermute(value, axis, pairs)


def from_partner(value):
    return exchange(value, "leaf", 1)


def after(value, *others):
    return lax.optimization_barrier((value, *others))[0]


def pick(halves, wanted, far_within):
    one, two = shape((1, COLS, 2 * RANK), BF16), shape((2, COLS, 2 * RANK), BF16)
    return call(
        select_kernel,
        [two, two, two, one, shape((3, COLS, 2 * RANK), BF16)],
        [VMEM] * 2 + [SMEM] * 2,
        (*halves, wanted, far_within),
        0.7,
        [pltpu.VMEM((16, COLS, 2 * RANK), BF16)],
        name="select",
    )


def exchanges(wide, steps, wanted, far_within):
    partner = from_partner(wide)
    total = steps[0]()
    partner = after(partner, total)
    chip = (wide[:COLS, POINTS:] + partner[:COLS, POINTS:])[None]
    rows = exchange(chip, "leaf", 8)
    pair = jnp.stack([wide[:, :POINTS], partner[:, :POINTS]])
    two = jnp.concatenate([chip, rows])
    rows = exchange(two, "leaf", 16)
    first = from_both_sides(pair, BOTH, 1, 2)
    total = steps[1](partner, total)
    rows = after(rows, total)
    four = jnp.concatenate([two, rows])
    columns = exchange(four, "leaf", 2)
    passed_first = from_partner(first)
    second = from_both_sides(pair, BOTH, 2, 2)
    total = steps[2](first, total)
    columns = after(columns, total)
    eight = jnp.concatenate([four, columns])
    columns = exchange(eight, "leaf", 4)
    passed_second = from_partner(second)
    total = steps[3](passed_first, total)
    columns = after(columns, total)
    *sends, inside = pick((eight, columns), wanted(total), far_within)
    arrived = [from_both_sides(sends[j - 1], BOTH, j, 32) for j in (1, 2, 3, 4)]
    total = steps[4](second, total)
    arrived = [after(a, total) for a in arrived]
    passed = from_partner(jnp.stack([arrived[j][1] for j in range(3)]))
    total = steps[5](passed_second, total)
    return (inside, *arrived, after(passed, total)), total


def local(
    observations,
    coordinates,
    proxies,
    noise_variance,
    ordering,
    near_list,
    far_within,
    far_across,
    couplings,
):
    leaves = lax.axis_size(BOTH)
    leaf_id = lax.axis_index(BOTH)
    core = leaf_id % 2
    offsets = jnp.array([1, 2, 3, -1, -2, 4, 5, -3, -4], jnp.int32) * (1 - 2 * core)
    targets = (leaf_id + offsets + leaves) % leaves
    flags = jnp.any(near_list[0][None, :] == targets[:, None], axis=1).astype(jnp.int32)
    noise = noise_variance[None, :]

    message, column = call(
        prepare_kernel,
        [shape((COLS + 16, POINTS), BF16), shape((3, POINTS, 128), F32)],
        [pl.BlockSpec(memory_space=pltpu.HBM)] * 3,
        (observations, ordering, coordinates),
        2.0,
        [
            pltpu.VMEM((POINTS, POINTS), BF16),
            pltpu.VMEM((COLS, POINTS), F32),
            pltpu.VMEM((1, POINTS), jnp.int32),
            pltpu.VMEM((3, POINTS), F32),
            pltpu.SemaphoreType.DMA((3,)),
        ],
        name="prepare",
    )
    basis, wide = call(
        basis_kernel,
        [shape((RANK, POINTS), BF16), shape((COLS + 16, POINTS + 2 * RANK), BF16)],
        [VMEM] * 2,
        (message, proxies[0].T),
        0.7,
        name="basis",
    )
    tile_shape, total_shape = shape((POINTS, POINTS), BF16), shape((POINTS, COLS), F32)
    tiles, asked = [], [jnp.stack([far_across[0], from_partner(far_across[0])]).reshape(1, 28)]

    def ask(bit, total):
        mine = after(asked[-1], total)
        asked.append(jnp.concatenate([mine, exchange(mine, "group", bit)]))

    def build_own():
        tile, total = call(
            own_tile_kernel, [tile_shape, total_shape], [VMEM] * 2, (wide, column), 2.0, name="own_tile"
        )
        tiles.append(tile)
        ask(1, total)
        return total

    def build_partner(partner, total):
        tile, total = call(
            partner_tile_kernel,
            [tile_shape, total_shape],
            [SMEM] + [VMEM] * 3,
            (flags, partner, column, total),
            2.0,
            name="partner_tile",
        )
        tiles.append(tile)
        ask(2, total)
        return total

    def build_pair(place, pair, total):
        tile, total = call(
            functools.partial(pair_tiles_kernel, place),
            [shape((2, POINTS, POINTS), BF16), total_shape],
            [SMEM] + [VMEM] * 3,
            (flags, pair, column, total),
            4.0,
            name="pair_tiles",
        )
        tiles.append(tile)
        if place == 1:
            ask(4, total)
        return total

    far, total = exchanges(
        wide,
        [build_own, build_partner]
        + [functools.partial(build_pair, place) for place in (1, 3, 5, 7)],
        lambda total: asked[-1].reshape(8 * 28),
        far_within,
    )
    field = shape((COLS, POINTS), F32)
    gain, residual, direction, wide = call(
        update_kernel,
        [field, field, field, shape((COLS, POINTS + 2 * RANK), BF16)],
        [VMEM] * 11,
        (observations, noise, *far, couplings, basis, total),
        1.5,
        name="update",
    )

    def apply_own():
        return call(
            apply_own_kernel, total_shape, [VMEM] * 2, (wide, tiles[0]), 0.7, name="apply_own"
        )

    def apply_near(at, place, count, block, total):
        return call(
            functools.partial(apply_near_kernel, ((place, count),)),
            total_shape,
            [SMEM] + [VMEM] * 3,
            (flags, block, tiles[at], total),
            0.7 * count,
            name="apply_near",
        )

    far, total = exchanges(
        wide,
        [apply_own, functools.partial(apply_near, 1, 0, 1)]
        + [functools.partial(apply_near, 2 + at, 1 + 2 * at, 2) for at in range(4)],
        lambda total: asked[-1].reshape(8 * 28),
        far_within,
    )
    residual = call(
        finish_kernel,
        field,
        [VMEM] * 12,
        (residual, direction, noise, *far, couplings, basis, total),
        1.0,
        name="finish",
    )
    return (gain, residual)


def solution(mesh):
    placed = (
        P(None, ("group", "leaf")),
        P(None, ("group", "leaf")),
        P(("group", "leaf"), None, None),
        P(("group", "leaf")),
        P(("group", "leaf"), None),
        P(("group", "leaf"), None),
        P(("group", "leaf"), None),
        P(("group", "leaf"), None, None),
        P(("group", "leaf"), None, None, None),
    )
    return jax.shard_map(
        local,
        mesh=mesh,
        in_specs=placed,
        out_specs=(P(None, ("group", "leaf")), P(None, ("group", "leaf"))),
        check_vma=False,
    )
```

```python
import functools

import jax
import jax.numpy as jnp
from jax import lax
from jax.experimental import pallas as pl
from jax.experimental.pallas import tpu as pltpu
from jax.sharding import PartitionSpec as P

ITERS = 2
COLS = 64
POINTS = 1024
RANK = 64
CHUNK = 256
STEP = 16

length_scale = 0.5
kernel_scale = 8.0
lower_bound = 0.5
upper_bound = 4.0
centre = (upper_bound + lower_bound) / 2.0
half_width = (upper_bound - lower_bound) / 2.0
SCALE = 1.4426950408889634 / length_scale
ratio_first = 1.0 / (centre / half_width)
ratio_second = 1.0 / (2.0 * centre / half_width - ratio_first)
ALONG = ratio_second * ratio_first
ACROSS = 2.0 * ratio_second / half_width

F32, BF16 = jnp.float32, jnp.bfloat16
LAST = (((1,), (1,)), ((), ()))
VMEM = pl.BlockSpec(memory_space=pltpu.VMEM)
SMEM = pl.BlockSpec(memory_space=pltpu.SMEM)
BOTH = ("group", "leaf")


def shape(dims, kind):
    return jax.ShapeDtypeStruct(dims, kind)


def call(body, outs, ins, args, cost, scratch=(), aliases=None, name=None):
    several = isinstance(outs, (list, tuple))
    return pl.pallas_call(
        body,
        out_shape=outs,
        in_specs=ins,
        out_specs=[VMEM] * len(outs) if several else VMEM,
        scratch_shapes=list(scratch),
        input_output_aliases=aliases or {},
        compiler_params=pltpu.CompilerParams(vmem_limit_bytes=20 * 2**20),
        cost_estimate=pl.CostEstimate(
            flops=int(cost * 1e9), bytes_accessed=int(cost * 1e5), transcendentals=0
        ),
        name=name,
    )(*args)


def distance_kernel(squared):
    kept = jnp.maximum(squared, 1e-30)
    return jnp.exp2(-(kept * lax.rsqrt(kept)))


def coordinate_rows(tail):
    parts = tail.astype(F32)
    return parts[0:3] + parts[3:6] + parts[6:9]


def prepare_kernel(obs_hbm, order_hbm, coord_hbm, message_ref, column_ref, onehot, obs_ref, order_ref, coord_ref, sems):
    loads = [
        pltpu.make_async_copy(order_hbm, order_ref, sems.at[0]),
        pltpu.make_async_copy(coord_hbm, coord_ref, sems.at[1]),
        pltpu.make_async_copy(obs_hbm, obs_ref, sems.at[2]),
    ]
    for load in loads:
        load.start()
    loads[0].wait()
    loads[1].wait()
    scaled = coord_ref[...] * SCALE
    high = scaled.astype(BF16)
    left = scaled - high.astype(F32)
    middle = left.astype(BF16)
    low = (left - middle.astype(F32)).astype(BF16)
    parts = jnp.concatenate(
        [high.astype(F32), middle.astype(F32), low.astype(F32), jnp.zeros((119, POINTS), F32)],
        axis=0,
    ).astype(BF16)
    order = jnp.broadcast_to(order_ref[...], (STEP, POINTS))
    slot = lax.broadcasted_iota(jnp.int32, (STEP, POINTS), 0)
    for first in range(0, POINTS, CHUNK):
        for row in range(first, first + CHUNK, STEP):
            onehot[row : row + STEP, :] = jnp.where(order == slot + row, 1.0, 0.0).astype(BF16)
        placed = lax.dot_general(
            onehot[first : first + CHUNK, :], parts, LAST, preferred_element_type=F32
        )
        column_ref[first : first + CHUNK, 0:3] = placed[:, 0:3] + placed[:, 3:6] + placed[:, 6:9]
        message_ref[COLS : COLS + 16, first : first + CHUNK] = placed.T[0:16, :].astype(BF16)
    loads[2].wait()
    message_ref[0:COLS, :] = (obs_ref[...] / centre).astype(BF16)


def half_of_chip(block):
    wide = jnp.concatenate([block, block], axis=1)
    lane = lax.broadcasted_iota(jnp.int32, (COLS, 2 * RANK), 1)
    core = lax.rem(lax.axis_index("leaf"), 2)
    return jnp.where(lane // RANK == core, wide, 0.0).astype(BF16)


def basis_kernel(message_ref, proxy_ref, basis_ref, wide_ref):
    rows = coordinate_rows(message_ref[COLS : COLS + 16, :])
    squared = None
    for c in range(3):
        apart = proxy_ref[:, c : c + 1] * SCALE - rows[c : c + 1, :]
        squared = apart * apart if squared is None else squared + apart * apart
    basis = distance_kernel(squared).astype(BF16)
    basis_ref[...] = basis
    wide_ref[:, 0:POINTS] = message_ref[...]
    wide_ref[0:COLS, POINTS:] = half_of_chip(
        lax.dot_general(message_ref[0:COLS, :], basis, LAST, preferred_element_type=F32)
    )
    wide_ref[COLS : COLS + 16, POINTS:] = jnp.zeros((16, 2 * RANK), BF16)


def fill_column(column_ref, filled):
    for c in range(3):
        for row in range(0, POINTS, CHUNK):
            filled[c, row : row + CHUNK, :] = jnp.broadcast_to(
                column_ref[row : row + CHUNK, c : c + 1], (CHUNK, 128)
            )


def build_and_apply(block, column_ref, tile_ref, total_ref, first_block):
    coords = coordinate_rows(block[COLS : COLS + 16, 0:POINTS])
    rows = [jnp.broadcast_to(coords[c : c + 1, :], (STEP, POINTS)) for c in range(3)]
    field = block[0:COLS, 0:POINTS]
    for first in range(0, POINTS, CHUNK):
        for row in range(first, first + CHUNK, STEP):
            pieces = []
            for lane in range(0, POINTS, 128):
                squared = None
                for c in range(3):
                    apart = column_ref[c, row : row + STEP, :] - rows[c][:, lane : lane + 128]
                    squared = apart * apart if squared is None else squared + apart * apart
                pieces.append(distance_kernel(squared).astype(BF16))
            tile_ref[row : row + STEP, :] = jnp.concatenate(pieces, axis=1)
        product = lax.dot_general(
            tile_ref[first : first + CHUNK, :], field, LAST, preferred_element_type=F32
        )
        if first_block:
            total_ref[first : first + CHUNK, :] = product
        else:
            total_ref[first : first + CHUNK, :] += product


def own_tile_kernel(own_ref, column_ref, own_tile, total_ref, filled):
    fill_column(column_ref, filled)
    build_and_apply(own_ref, filled, own_tile, total_ref, True)


def partner_tile_kernel(flag_ref, partner_ref, column_ref, total_in, tile_ref, total_ref, filled):
    total_ref[...] = total_in[...]

    @pl.when(flag_ref[0] != 0)
    def _():
        fill_column(column_ref, filled)
        build_and_apply(partner_ref, filled, tile_ref, total_ref, False)


def pair_tiles_kernel(place, flag_ref, *refs):
    *refs, filled = refs
    count = (len(refs) - 3) // 2
    column_ref, total_in, total_ref = refs[count], refs[count + 1], refs[-1]
    total_ref[...] = total_in[...]
    fill_column(column_ref, filled)
    for which in range(count):
        pair_ref, tiles_ref = refs[which], refs[count + 2 + which]

        @pl.loop(0, 2)
        def _(at, which=which, pair_ref=pair_ref, tiles_ref=tiles_ref):
            @pl.when(flag_ref[place + 2 * which + at] != 0)
            def _():
                build_and_apply(pair_ref.at[at], filled, tiles_ref.at[at], total_ref, False)


def apply_own_kernel(wide_ref, tile_ref, total_ref):
    total_ref[...] = lax.dot_general(
        tile_ref[...], wide_ref[:, 0:POINTS], LAST, preferred_element_type=F32
    )


def apply_near_kernel(places, flag_ref, *refs):
    count = len(places)
    total_ref = refs[-1]
    total_ref[...] = refs[-2][...]
    for which, (place, blocks) in enumerate(places):
        for at in range(blocks):

            @pl.when(flag_ref[place + at] != 0)
            def _(which=which, at=at, blocks=blocks):
                block, tile = refs[which], refs[count + which]
                if blocks == 2:
                    block, tile = block.at[at], tile.at[at]
                total_ref[...] += lax.dot_general(
                    tile[...], block[0:COLS, 0:POINTS], LAST, preferred_element_type=F32
                )


def select_kernel(*refs):
    gathered, wanted, within_ref = refs[0:2], refs[2], refs[3]
    sends, inside_ref, held = refs[4:8], refs[8], refs[9]
    held[0:8] = gathered[0][...]
    held[8:16] = gathered[1][...]
    mine = lax.axis_index("leaf")
    my_y, my_x, my_core = mine // 8, lax.rem(mine // 2, 4), lax.rem(mine, 2)
    low_half = lax.broadcasted_iota(jnp.int32, (COLS, 2 * RANK), 1) < RANK

    def pair(first, second):
        halves = []
        for leaf, half in ((first, 0), (second, 1)):
            y, x, core = leaf // 8, lax.rem(leaf // 2, 4), lax.rem(leaf, 2)
            dx, dy = x ^ my_x, y ^ my_y
            at = (dx ^ (dx // 2)) * 4 + (dy ^ (dy // 2))
            block = held[at].astype(F32)
            turned = jnp.concatenate([block[:, RANK:], block[:, :RANK]], axis=1)
            same = jnp.full((COLS, 2 * RANK), core, jnp.int32) == half
            halves.append(jnp.where(same, block, turned))
        return jnp.where(low_half, halves[0], halves[1]).astype(BF16)

    for j in (1, 2, 3, 4):
        k = jnp.where(my_core == 0, j - 1, 7 - j)
        for who in range(1 if j == 4 else 2):
            at = (2 * (j - 1) + who) * 14 + 2 * k
            sends[j - 1][who] = pair(wanted[at], wanted[at + 1])
    for k in range(3):
        inside_ref[k] = pair(within_ref[0, 2 * k], within_ref[0, 2 * k + 1])


def kernel_part(inside_ref, arrived, passed_ref, coupling_ref, basis_ref, total_ref):
    core = lax.rem(lax.axis_index("leaf"), 2)
    spread = None

    def add(spread, source, first):
        for a in range(2):
            half = source.astype(F32)[:, a * RANK : a * RANK + RANK].astype(BF16)
            term = lax.dot_general(half, coupling_ref[0, first + a], LAST, preferred_element_type=F32)
            spread = term if spread is None else spread + term
        return spread

    for k in range(3):
        spread = add(spread, inside_ref[k], 2 * k)
    for j in (1, 2, 3):
        near, away = 6 + 2 * (j - 1), 6 + 2 * (7 - j)
        spread = add(spread, arrived[j - 1][0], jnp.where(core == 0, near, away))
        spread = add(spread, passed_ref[j - 1], jnp.where(core == 0, away, near))
    spread = add(spread, arrived[3][0], 6 + 2 * 3)
    far = jnp.dot(spread.astype(BF16), basis_ref[...], preferred_element_type=F32)
    return (total_ref[...].T + far) / kernel_scale


def update_kernel(*refs):
    obs_ref, noise_ref, inside_ref, arrived, passed_ref = refs[0], refs[1], refs[2], refs[3:7], refs[7]
    coupling_ref, basis_ref, total_ref = refs[8:11]
    gain_ref, residual_ref, direction_ref, wide_ref = refs[11:15]
    right_side = obs_ref[...]
    direction = right_side / centre
    applied = noise_ref[...] * direction + kernel_part(
        inside_ref, arrived, passed_ref, coupling_ref, basis_ref, total_ref
    )
    residual = right_side - applied
    later = ALONG * direction + ACROSS * residual
    rounded = later.astype(BF16)
    wide_ref[:, 0:POINTS] = rounded
    wide_ref[:, POINTS:] = half_of_chip(
        lax.dot_general(rounded, basis_ref[...], LAST, preferred_element_type=F32)
    )
    gain_ref[...] = direction + later
    residual_ref[...] = residual
    direction_ref[...] = later


def finish_kernel(*refs):
    before_ref, direction_ref, noise_ref, inside_ref, arrived, passed_ref = (*refs[0:4], refs[4:8], refs[8])
    coupling_ref, basis_ref, total_ref = refs[9:12]
    applied = noise_ref[...] * direction_ref[...] + kernel_part(
        inside_ref, arrived, passed_ref, coupling_ref, basis_ref, total_ref
    )
    refs[12][...] = before_ref[...] - applied


def from_ahead(value, axis, steps):
    count = lax.axis_size(axis)
    return lax.ppermute(value, axis, [(s, (s - steps) % count) for s in range(count)])


def exchange(value, axis, distance):
    count = lax.axis_size(axis)
    return lax.ppermute(value, axis, [(s, s ^ distance) for s in range(count)])


def from_both_sides(value, axis, chips, per_chip):
    count = lax.axis_size(axis)
    pairs = []
    for s in range(count):
        steps = -chips * per_chip if s % 2 == 0 else chips * per_chip
        pairs.append((s, (s + steps) % count))
    return lax.ppermute(value, axis, pairs)


def from_partner(value):
    return exchange(value, "leaf", 1)


def after(value, *others):
    return lax.optimization_barrier((value, *others))[0]


def pick(halves, wanted, far_within):
    one, two = shape((1, COLS, 2 * RANK), BF16), shape((2, COLS, 2 * RANK), BF16)
    return call(
        select_kernel,
        [two, two, two, one, shape((3, COLS, 2 * RANK), BF16)],
        [VMEM] * 2 + [SMEM] * 2,
        (*halves, wanted, far_within),
        0.7,
        [pltpu.VMEM((16, COLS, 2 * RANK), BF16)],
        name="select",
    )


def exchanges(wide, steps, wanted, far_within):
    partner = from_partner(wide)
    total = steps[0]()
    partner = after(partner, total)
    chip = (wide[:COLS, POINTS:] + partner[:COLS, POINTS:])[None]
    rows = exchange(chip, "leaf", 8)
    total = steps[1](partner, total)
    rows = after(rows, total)
    two = jnp.concatenate([chip, rows])
    rows = exchange(two, "leaf", 24)
    pair = after(jnp.stack([wide[:, :POINTS], partner[:, :POINTS]]), two)
    first = from_both_sides(pair, BOTH, 1, 2)
    four = jnp.concatenate([two, rows])
    columns = exchange(four, "leaf", 2)
    first = after(first, four)
    second = from_both_sides(first, BOTH, 1, 2)
    passed_first = from_partner(first)
    total = steps[2](first, total)
    columns = after(columns, total)
    eight = jnp.concatenate([four, columns])
    columns = exchange(eight, "leaf", 6)
    passed_second = from_partner(second)
    total = steps[3](passed_first, total)
    columns = after(columns, total)
    *sends, inside = pick((eight, columns), wanted, far_within)
    arrived = [from_both_sides(sends[j - 1], BOTH, j, 32) for j in (1, 2, 3, 4)]
    total = steps[4](second, passed_second, total)
    arrived = [after(a, total) for a in arrived]
    passed = from_partner(after(jnp.stack([arrived[j][1] for j in range(3)]), arrived[3]))
    return (inside, *arrived, passed), total


def local(
    observations,
    coordinates,
    proxies,
    noise_variance,
    ordering,
    near_list,
    far_within,
    far_across,
    couplings,
):
    leaves = lax.axis_size(BOTH)
    leaf_id = lax.axis_index(BOTH)
    core = leaf_id % 2
    listed = jnp.concatenate([far_across, from_partner(far_across)])
    asked = jnp.stack([from_both_sides(listed, BOTH, -j, 32) for j in (1, 2, 3, 4)]).reshape(112)
    offsets = jnp.array([1, 2, 3, -1, -2, 4, 5, -3, -4], jnp.int32) * (1 - 2 * core)
    targets = (leaf_id + offsets + leaves) % leaves
    flags = jnp.any(near_list[0][None, :] == targets[:, None], axis=1).astype(jnp.int32)
    noise = noise_variance[None, :]

    message, column = call(
        prepare_kernel,
        [shape((COLS + 16, POINTS), BF16), shape((POINTS, 128), F32)],
        [pl.BlockSpec(memory_space=pltpu.HBM)] * 3,
        (observations, ordering, coordinates),
        2.0,
        [
            pltpu.VMEM((POINTS, POINTS), BF16),
            pltpu.VMEM((COLS, POINTS), F32),
            pltpu.VMEM((1, POINTS), jnp.int32),
            pltpu.VMEM((3, POINTS), F32),
            pltpu.SemaphoreType.DMA((3,)),
        ],
        name="prepare",
    )
    basis, wide = call(
        basis_kernel,
        [shape((RANK, POINTS), BF16), shape((COLS + 16, POINTS + 2 * RANK), BF16)],
        [VMEM] * 2,
        (message, proxies[0].T),
        0.7,
        name="basis",
    )
    tile_shape, total_shape = shape((POINTS, POINTS), BF16), shape((POINTS, COLS), F32)
    tiles, filled = [], [pltpu.VMEM((3, POINTS, 128), F32)]

    def build_own():
        tile, total = call(
            own_tile_kernel, [tile_shape, total_shape], [VMEM] * 2, (wide, column), 2.0, filled, name="own_tile"
        )
        tiles.append(tile)
        return total

    def build_partner(partner, total):
        tile, total = call(
            partner_tile_kernel,
            [tile_shape, total_shape],
            [SMEM] + [VMEM] * 3,
            (flags, partner, column, total),
            2.0,
            filled,
            name="partner_tile",
        )
        tiles.append(tile)
        return total

    def build_pairs(place, *pairs_total):
        *pairs, total = pairs_total
        *built, total = call(
            functools.partial(pair_tiles_kernel, place),
            [shape((2, POINTS, POINTS), BF16)] * len(pairs) + [total_shape],
            [SMEM] + [VMEM] * (len(pairs) + 2),
            (flags, *pairs, column, total),
            4.0 * len(pairs),
            filled,
            name="pair_tiles",
        )
        tiles.extend(built)
        return total

    far, total = exchanges(
        wide,
        [build_own, build_partner]
        + [functools.partial(build_pairs, place) for place in (1, 3, 5)],
        asked,
        far_within,
    )
    field = shape((COLS, POINTS), F32)
    gain, residual, direction, wide = call(
        update_kernel,
        [field, field, field, shape((COLS, POINTS + 2 * RANK), BF16)],
        [VMEM] * 11,
        (observations, noise, *far, couplings, basis, total),
        1.5,
        name="update",
    )

    def apply_own():
        return call(
            apply_own_kernel, total_shape, [VMEM] * 2, (wide, tiles[0]), 0.7, name="apply_own"
        )

    def apply_near(places, *blocks_total):
        *blocks, total = blocks_total
        matching = [tiles[1 + (place + 1) // 2] for place, _ in places]
        return call(
            functools.partial(apply_near_kernel, places),
            total_shape,
            [SMEM] + [VMEM] * (2 * len(places) + 1),
            (flags, *blocks, *matching, total),
            0.7 * sum(count for _, count in places),
            name="apply_near",
        )

    far, total = exchanges(
        wide,
        [apply_own]
        + [
            functools.partial(apply_near, places)
            for places in (((0, 1),), ((1, 2),), ((3, 2),), ((5, 2), (7, 2)))
        ],
        asked,
        far_within,
    )
    residual = call(
        finish_kernel,
        field,
        [VMEM] * 12,
        (residual, direction, noise, *far, couplings, basis, total),
        1.0,
        name="finish",
    )
    return (gain, residual)


def solution(mesh):
    placed = (
        P(None, ("group", "leaf")),
        P(None, ("group", "leaf")),
        P(("group", "leaf"), None, None),
        P(("group", "leaf")),
        P(("group", "leaf"), None),
        P(("group", "leaf"), None),
        P(("group", "leaf"), None),
        P(("group", "leaf"), None, None),
        P(("group", "leaf"), None, None, None),
    )
    return jax.shard_map(
        local,
        mesh=mesh,
        in_specs=placed,
        out_specs=(P(None, ("group", "leaf")), P(None, ("group", "leaf"))),
        check_vma=False,
    )
```

```python
import functools

import jax
import jax.numpy as jnp
from jax import lax
from jax.experimental import pallas as pl
from jax.experimental.pallas import tpu as pltpu
from jax.sharding import PartitionSpec as P

ITERS = 2
COLS = 64
POINTS = 1024
RANK = 64
CHUNK = 256
STEP = 16

length_scale = 0.5
kernel_scale = 8.0
lower_bound = 0.5
upper_bound = 4.0
centre = (upper_bound + lower_bound) / 2.0
half_width = (upper_bound - lower_bound) / 2.0
SCALE = 1.4426950408889634 / length_scale
ratio_first = 1.0 / (centre / half_width)
ratio_second = 1.0 / (2.0 * centre / half_width - ratio_first)
ALONG = ratio_second * ratio_first
ACROSS = 2.0 * ratio_second / half_width

F32, BF16 = jnp.float32, jnp.bfloat16
LAST = (((1,), (1,)), ((), ()))
VMEM = pl.BlockSpec(memory_space=pltpu.VMEM)
SMEM = pl.BlockSpec(memory_space=pltpu.SMEM)
BOTH = ("group", "leaf")


def shape(dims, kind):
    return jax.ShapeDtypeStruct(dims, kind)


def call(body, outs, ins, args, cost, scratch=(), aliases=None, name=None):
    several = isinstance(outs, (list, tuple))
    return pl.pallas_call(
        body,
        out_shape=outs,
        in_specs=ins,
        out_specs=[VMEM] * len(outs) if several else VMEM,
        scratch_shapes=list(scratch),
        input_output_aliases=aliases or {},
        compiler_params=pltpu.CompilerParams(vmem_limit_bytes=20 * 2**20),
        cost_estimate=pl.CostEstimate(
            flops=int(cost * 1e9), bytes_accessed=int(cost * 1e5), transcendentals=0
        ),
        name=name,
    )(*args)


def distance_kernel(squared):
    kept = jnp.maximum(squared, 1e-30)
    return jnp.exp2(-(kept * lax.rsqrt(kept)))


def coordinate_rows(tail):
    parts = tail.astype(F32)
    return parts[0:3] + parts[3:6] + parts[6:9]


def prepare_kernel(obs_hbm, order_hbm, coord_hbm, message_ref, column_ref, onehot, obs_ref, order_ref, coord_ref, sems):
    loads = [
        pltpu.make_async_copy(order_hbm, order_ref, sems.at[0]),
        pltpu.make_async_copy(coord_hbm, coord_ref, sems.at[1]),
        pltpu.make_async_copy(obs_hbm, obs_ref, sems.at[2]),
    ]
    for load in loads:
        load.start()
    loads[0].wait()
    loads[1].wait()
    scaled = coord_ref[...] * SCALE
    high = scaled.astype(BF16)
    left = scaled - high.astype(F32)
    middle = left.astype(BF16)
    low = (left - middle.astype(F32)).astype(BF16)
    parts = jnp.concatenate(
        [high.astype(F32), middle.astype(F32), low.astype(F32), jnp.zeros((119, POINTS), F32)],
        axis=0,
    ).astype(BF16)
    order = jnp.broadcast_to(order_ref[...], (STEP, POINTS))
    slot = lax.broadcasted_iota(jnp.int32, (STEP, POINTS), 0)
    for first in range(0, POINTS, CHUNK):
        for row in range(first, first + CHUNK, STEP):
            onehot[row : row + STEP, :] = jnp.where(order == slot + row, 1.0, 0.0).astype(BF16)
        placed = lax.dot_general(
            onehot[first : first + CHUNK, :], parts, LAST, preferred_element_type=F32
        )
        column_ref[first : first + CHUNK, 0:3] = placed[:, 0:3] + placed[:, 3:6] + placed[:, 6:9]
        message_ref[COLS : COLS + 16, first : first + CHUNK] = placed.T[0:16, :].astype(BF16)
    loads[2].wait()
    message_ref[0:COLS, :] = (obs_ref[...] / centre).astype(BF16)


def half_of_chip(block):
    wide = jnp.concatenate([block, block], axis=1)
    lane = lax.broadcasted_iota(jnp.int32, (COLS, 2 * RANK), 1)
    core = lax.rem(lax.axis_index("leaf"), 2)
    return jnp.where(lane // RANK == core, wide, 0.0).astype(BF16)


def basis_kernel(message_ref, proxy_ref, basis_ref, wide_ref):
    rows = coordinate_rows(message_ref[COLS : COLS + 16, :])
    squared = None
    for c in range(3):
        apart = proxy_ref[:, c : c + 1] * SCALE - rows[c : c + 1, :]
        squared = apart * apart if squared is None else squared + apart * apart
    basis = distance_kernel(squared).astype(BF16)
    basis_ref[...] = basis
    wide_ref[:, 0:POINTS] = message_ref[...]
    wide_ref[0:COLS, POINTS:] = half_of_chip(
        lax.dot_general(message_ref[0:COLS, :], basis, LAST, preferred_element_type=F32)
    )
    wide_ref[COLS : COLS + 16, POINTS:] = jnp.zeros((16, 2 * RANK), BF16)


def fill_column(column_ref, filled):
    for c in range(3):
        for row in range(0, POINTS, CHUNK):
            filled[c, row : row + CHUNK, :] = jnp.broadcast_to(
                column_ref[row : row + CHUNK, c : c + 1], (CHUNK, 128)
            )


def build_and_apply(block, column_ref, tile_ref, total_ref, first_block):
    coords = coordinate_rows(block[COLS : COLS + 16, 0:POINTS])
    rows = [jnp.broadcast_to(coords[c : c + 1, :], (STEP, POINTS)) for c in range(3)]
    field = block[0:COLS, 0:POINTS]
    for first in range(0, POINTS, CHUNK):
        for row in range(first, first + CHUNK, STEP):
            pieces = []
            for lane in range(0, POINTS, 128):
                squared = None
                for c in range(3):
                    apart = column_ref[c, row : row + STEP, :] - rows[c][:, lane : lane + 128]
                    squared = apart * apart if squared is None else squared + apart * apart
                pieces.append(distance_kernel(squared).astype(BF16))
            tile_ref[row : row + STEP, :] = jnp.concatenate(pieces, axis=1)
        product = lax.dot_general(
            tile_ref[first : first + CHUNK, :], field, LAST, preferred_element_type=F32
        )
        if first_block:
            total_ref[first : first + CHUNK, :] = product
        else:
            total_ref[first : first + CHUNK, :] += product


def own_tile_kernel(own_ref, column_ref, own_tile, total_ref, filled):
    fill_column(column_ref, filled)
    build_and_apply(own_ref, filled, own_tile, total_ref, True)


def partner_tile_kernel(flag_ref, partner_ref, column_ref, total_in, tile_ref, total_ref, filled):
    total_ref[...] = total_in[...]

    @pl.when(flag_ref[0] != 0)
    def _():
        fill_column(column_ref, filled)
        build_and_apply(partner_ref, filled, tile_ref, total_ref, False)


def pair_tiles_kernel(place, flag_ref, *refs):
    *refs, filled = refs
    count = (len(refs) - 3) // 2
    column_ref, total_in, total_ref = refs[count], refs[count + 1], refs[-1]
    total_ref[...] = total_in[...]
    fill_column(column_ref, filled)
    for which in range(count):
        pair_ref, tiles_ref = refs[which], refs[count + 2 + which]

        @pl.loop(0, 2)
        def _(at, which=which, pair_ref=pair_ref, tiles_ref=tiles_ref):
            @pl.when(flag_ref[place + 2 * which + at] != 0)
            def _():
                build_and_apply(pair_ref.at[at], filled, tiles_ref.at[at], total_ref, False)


def apply_own_kernel(wide_ref, tile_ref, total_ref):
    total_ref[...] = lax.dot_general(
        tile_ref[...], wide_ref[:, 0:POINTS], LAST, preferred_element_type=F32
    )


def apply_near_kernel(places, flag_ref, *refs):
    count = len(places)
    total_ref = refs[-1]
    total_ref[...] = refs[-2][...]
    for which, (place, blocks) in enumerate(places):
        for at in range(blocks):

            @pl.when(flag_ref[place + at] != 0)
            def _(which=which, at=at, blocks=blocks):
                block, tile = refs[which], refs[count + which]
                if blocks == 2:
                    block, tile = block.at[at], tile.at[at]
                total_ref[...] += lax.dot_general(
                    tile[...], block[0:COLS, 0:POINTS], LAST, preferred_element_type=F32
                )


def select_kernel(*refs):
    gathered, wanted, within_ref = refs[0:2], refs[2], refs[3]
    sends, inside_ref, held = refs[4:8], refs[8], refs[9]
    held[0:8] = gathered[0][...]
    held[8:16] = gathered[1][...]
    mine = lax.axis_index("leaf")
    my_y, my_x, my_core = mine // 8, lax.rem(mine // 2, 4), lax.rem(mine, 2)
    low_half = lax.broadcasted_iota(jnp.int32, (COLS, 2 * RANK), 1) < RANK

    def pair(first, second):
        halves = []
        for leaf, half in ((first, 0), (second, 1)):
            y, x, core = leaf // 8, lax.rem(leaf // 2, 4), lax.rem(leaf, 2)
            dx, dy = x ^ my_x, y ^ my_y
            at = (dx ^ (dx // 2)) * 4 + (dy ^ (dy // 2))
            block = held[at].astype(F32)
            turned = jnp.concatenate([block[:, RANK:], block[:, :RANK]], axis=1)
            same = jnp.full((COLS, 2 * RANK), core, jnp.int32) == half
            halves.append(jnp.where(same, block, turned))
        return jnp.where(low_half, halves[0], halves[1]).astype(BF16)

    for j in (1, 2, 3, 4):
        k = jnp.where(my_core == 0, j - 1, 7 - j)
        for who in range(1 if j == 4 else 2):
            at = (2 * (j - 1) + who) * 14 + 2 * k
            sends[j - 1][who] = pair(wanted[at], wanted[at + 1])
    for k in range(3):
        inside_ref[k] = pair(within_ref[0, 2 * k], within_ref[0, 2 * k + 1])


def kernel_part(inside_ref, arrived, passed_ref, coupling_ref, basis_ref, total_ref):
    core = lax.rem(lax.axis_index("leaf"), 2)
    spread = None

    def add(spread, source, first):
        for a in range(2):
            half = source.astype(F32)[:, a * RANK : a * RANK + RANK].astype(BF16)
            term = lax.dot_general(half, coupling_ref[0, first + a], LAST, preferred_element_type=F32)
            spread = term if spread is None else spread + term
        return spread

    for k in range(3):
        spread = add(spread, inside_ref[k], 2 * k)
    for j in (1, 2, 3):
        near, away = 6 + 2 * (j - 1), 6 + 2 * (7 - j)
        spread = add(spread, arrived[j - 1][0], jnp.where(core == 0, near, away))
        spread = add(spread, passed_ref[j - 1], jnp.where(core == 0, away, near))
    spread = add(spread, arrived[3][0], 6 + 2 * 3)
    far = jnp.dot(spread.astype(BF16), basis_ref[...], preferred_element_type=F32)
    return (total_ref[...].T + far) / kernel_scale


def update_kernel(*refs):
    obs_ref, noise_ref, inside_ref, arrived, passed_ref = refs[0], refs[1], refs[2], refs[3:7], refs[7]
    coupling_ref, basis_ref, total_ref = refs[8:11]
    gain_ref, residual_ref, direction_ref, wide_ref = refs[11:15]
    right_side = obs_ref[...]
    direction = right_side / centre
    applied = noise_ref[...] * direction + kernel_part(
        inside_ref, arrived, passed_ref, coupling_ref, basis_ref, total_ref
    )
    residual = right_side - applied
    later = ALONG * direction + ACROSS * residual
    rounded = later.astype(BF16)
    wide_ref[:, 0:POINTS] = rounded
    wide_ref[:, POINTS:] = half_of_chip(
        lax.dot_general(rounded, basis_ref[...], LAST, preferred_element_type=F32)
    )
    gain_ref[...] = direction + later
    residual_ref[...] = residual
    direction_ref[...] = later


def finish_kernel(*refs):
    before_ref, direction_ref, noise_ref, inside_ref, arrived, passed_ref = (*refs[0:4], refs[4:8], refs[8])
    coupling_ref, basis_ref, total_ref = refs[9:12]
    applied = noise_ref[...] * direction_ref[...] + kernel_part(
        inside_ref, arrived, passed_ref, coupling_ref, basis_ref, total_ref
    )
    refs[12][...] = before_ref[...] - applied


def from_ahead(value, axis, steps):
    count = lax.axis_size(axis)
    return lax.ppermute(value, axis, [(s, (s - steps) % count) for s in range(count)])


def exchange(value, axis, distance):
    count = lax.axis_size(axis)
    return lax.ppermute(value, axis, [(s, s ^ distance) for s in range(count)])


def from_both_sides(value, axis, chips, per_chip):
    count = lax.axis_size(axis)
    pairs = []
    for s in range(count):
        steps = -chips * per_chip if s % 2 == 0 else chips * per_chip
        pairs.append((s, (s + steps) % count))
    return lax.ppermute(value, axis, pairs)


def from_partner(value):
    return exchange(value, "leaf", 1)


def after(value, *others):
    return lax.optimization_barrier((value, *others))[0]


def pick(halves, wanted, far_within):
    one, two = shape((1, COLS, 2 * RANK), BF16), shape((2, COLS, 2 * RANK), BF16)
    return call(
        select_kernel,
        [two, two, two, one, shape((3, COLS, 2 * RANK), BF16)],
        [VMEM] * 2 + [SMEM] * 2,
        (*halves, wanted, far_within),
        0.7,
        [pltpu.VMEM((16, COLS, 2 * RANK), BF16)],
        name="select",
    )


def exchanges(wide, steps, wanted, far_within, after):
    partner = from_partner(wide)
    total = steps[0]()
    partner = after(partner, total)
    chip = (wide[:COLS, POINTS:] + partner[:COLS, POINTS:])[None]
    rows = exchange(chip, "leaf", 8)
    total = steps[1](partner, total)
    rows = after(rows, total)
    two = jnp.concatenate([chip, rows])
    rows = exchange(two, "leaf", 24)
    pair = after(jnp.stack([wide[:, :POINTS], partner[:, :POINTS]]), two)
    first = from_both_sides(pair, BOTH, 1, 2)
    four = jnp.concatenate([two, rows])
    columns = exchange(four, "leaf", 2)
    first = after(first, four)
    second = from_both_sides(first, BOTH, 1, 2)
    passed_first = from_partner(first)
    total = steps[2](first, total)
    columns = after(columns, total)
    eight = jnp.concatenate([four, columns])
    columns = exchange(eight, "leaf", 6)
    passed_second = from_partner(second)
    total = steps[3](passed_first, total)
    columns = after(columns, total)
    *sends, inside = pick((eight, columns), wanted, far_within)
    arrived = [from_both_sides(sends[j - 1], BOTH, j, 32) for j in (1, 2, 3, 4)]
    total = steps[4](second, passed_second, total)
    arrived = [after(a, total) for a in arrived]
    passed = from_partner(after(jnp.stack([arrived[j][1] for j in range(3)]), arrived[3]))
    return (inside, *arrived, passed), total


def local(
    observations,
    coordinates,
    proxies,
    noise_variance,
    ordering,
    near_list,
    far_within,
    far_across,
    couplings,
):
    leaves = lax.axis_size(BOTH)
    leaf_id = lax.axis_index(BOTH)
    core = leaf_id % 2
    listed = jnp.concatenate([far_across, from_partner(far_across)])
    asked = jnp.stack([from_both_sides(listed, BOTH, -j, 32) for j in (1, 2, 3, 4)]).reshape(112)
    offsets = jnp.array([1, 2, 3, -1, -2, 4, 5, -3, -4], jnp.int32) * (1 - 2 * core)
    targets = (leaf_id + offsets + leaves) % leaves
    flags = jnp.any(near_list[0][None, :] == targets[:, None], axis=1).astype(jnp.int32)
    noise = noise_variance[None, :]

    message, column = call(
        prepare_kernel,
        [shape((COLS + 16, POINTS), BF16), shape((POINTS, 128), F32)],
        [pl.BlockSpec(memory_space=pltpu.HBM)] * 3,
        (observations, ordering, coordinates),
        2.0,
        [
            pltpu.VMEM((POINTS, POINTS), BF16),
            pltpu.VMEM((COLS, POINTS), F32),
            pltpu.VMEM((1, POINTS), jnp.int32),
            pltpu.VMEM((3, POINTS), F32),
            pltpu.SemaphoreType.DMA((3,)),
        ],
        name="prepare",
    )
    basis, wide = call(
        basis_kernel,
        [shape((RANK, POINTS), BF16), shape((COLS + 16, POINTS + 2 * RANK), BF16)],
        [VMEM] * 2,
        (message, proxies[0].T),
        0.7,
        name="basis",
    )
    tile_shape, total_shape = shape((POINTS, POINTS), BF16), shape((POINTS, COLS), F32)
    tiles, filled = [], [pltpu.VMEM((3, POINTS, 128), F32)]

    def build_own():
        tile, total = call(
            own_tile_kernel, [tile_shape, total_shape], [VMEM] * 2, (wide, column), 2.0, filled, name="own_tile"
        )
        tiles.append(tile)
        return total

    def build_partner(partner, total):
        tile, total = call(
            partner_tile_kernel,
            [tile_shape, total_shape],
            [SMEM] + [VMEM] * 3,
            (flags, partner, column, total),
            2.0,
            filled,
            name="partner_tile",
        )
        tiles.append(tile)
        return total

    def build_pairs(place, *pairs_total):
        *pairs, total = pairs_total
        *built, total = call(
            functools.partial(pair_tiles_kernel, place),
            [shape((2, POINTS, POINTS), BF16)] * len(pairs) + [total_shape],
            [SMEM] + [VMEM] * (len(pairs) + 2),
            (flags, *pairs, column, total),
            4.0 * len(pairs),
            filled,
            name="pair_tiles",
        )
        tiles.extend(built)
        return total

    far, total = exchanges(
        wide,
        [build_own, build_partner]
        + [functools.partial(build_pairs, place) for place in (1, 3, 5)],
        asked,
        far_within,
        after,
    )
    field = shape((COLS, POINTS), F32)
    gain, residual, direction, wide = call(
        update_kernel,
        [field, field, field, shape((COLS, POINTS + 2 * RANK), BF16)],
        [VMEM] * 11,
        (observations, noise, *far, couplings, basis, total),
        1.5,
        name="update",
    )

    def apply_own():
        return call(
            apply_own_kernel, total_shape, [VMEM] * 2, (wide, tiles[0]), 0.7, name="apply_own"
        )

    def apply_near(places, *blocks_total):
        *blocks, total = blocks_total
        matching = [tiles[1 + (place + 1) // 2] for place, _ in places]
        return call(
            functools.partial(apply_near_kernel, places),
            total_shape,
            [SMEM] + [VMEM] * (2 * len(places) + 1),
            (flags, *blocks, *matching, total),
            0.7 * sum(count for _, count in places),
            name="apply_near",
        )

    far, total = exchanges(
        wide,
        [apply_own]
        + [
            functools.partial(apply_near, places)
            for places in (((0, 1),), ((1, 2),), ((3, 2),), ((5, 2), (7, 2)))
        ],
        asked,
        far_within,
        lambda value, *others: value,
    )
    residual = call(
        finish_kernel,
        field,
        [VMEM] * 12,
        (residual, direction, noise, *far, couplings, basis, total),
        1.0,
        name="finish",
    )
    return (gain, residual)


def solution(mesh):
    placed = (
        P(None, ("group", "leaf")),
        P(None, ("group", "leaf")),
        P(("group", "leaf"), None, None),
        P(("group", "leaf")),
        P(("group", "leaf"), None),
        P(("group", "leaf"), None),
        P(("group", "leaf"), None),
        P(("group", "leaf"), None, None),
        P(("group", "leaf"), None, None, None),
    )
    return jax.shard_map(
        local,
        mesh=mesh,
        in_specs=placed,
        out_specs=(P(None, ("group", "leaf")), P(None, ("group", "leaf"))),
        check_vma=False,
    )
```

```python
import functools

import jax
import jax.numpy as jnp
from jax import lax
from jax.experimental import pallas as pl
from jax.experimental.pallas import tpu as pltpu
from jax.sharding import PartitionSpec as P

ITERS = 2
COLS = 64
POINTS = 1024
RANK = 64
CHUNK = 256
STEP = 16

length_scale = 0.5
kernel_scale = 8.0
lower_bound = 0.5
upper_bound = 4.0
centre = (upper_bound + lower_bound) / 2.0
half_width = (upper_bound - lower_bound) / 2.0
SCALE = 1.4426950408889634 / length_scale
ratio_first = 1.0 / (centre / half_width)
ratio_second = 1.0 / (2.0 * centre / half_width - ratio_first)
ALONG = ratio_second * ratio_first
ACROSS = 2.0 * ratio_second / half_width

F32, BF16 = jnp.float32, jnp.bfloat16
LAST = (((1,), (1,)), ((), ()))
VMEM = pl.BlockSpec(memory_space=pltpu.VMEM)
SMEM = pl.BlockSpec(memory_space=pltpu.SMEM)
BOTH = ("group", "leaf")


def shape(dims, kind):
    return jax.ShapeDtypeStruct(dims, kind)


def call(body, outs, ins, args, cost, scratch=(), aliases=None, name=None):
    several = isinstance(outs, (list, tuple))
    return pl.pallas_call(
        body,
        out_shape=outs,
        in_specs=ins,
        out_specs=[VMEM] * len(outs) if several else VMEM,
        scratch_shapes=list(scratch),
        input_output_aliases=aliases or {},
        compiler_params=pltpu.CompilerParams(vmem_limit_bytes=20 * 2**20),
        cost_estimate=pl.CostEstimate(
            flops=int(cost * 1e9), bytes_accessed=int(cost * 1e5), transcendentals=0
        ),
        name=name,
    )(*args)


def distance_kernel(squared):
    kept = jnp.maximum(squared, 1e-30)
    return jnp.exp2(-(kept * lax.rsqrt(kept)))


def coordinate_rows(tail):
    parts = tail.astype(F32)
    return parts[0:3] + parts[3:6] + parts[6:9]


def prepare_kernel(obs_hbm, order_hbm, coord_hbm, message_ref, column_ref, onehot, obs_ref, order_ref, coord_ref, sems):
    loads = [
        pltpu.make_async_copy(order_hbm, order_ref, sems.at[0]),
        pltpu.make_async_copy(coord_hbm, coord_ref, sems.at[1]),
        pltpu.make_async_copy(obs_hbm, obs_ref, sems.at[2]),
    ]
    for load in loads:
        load.start()
    loads[0].wait()
    loads[1].wait()
    scaled = coord_ref[...] * SCALE
    high = scaled.astype(BF16)
    left = scaled - high.astype(F32)
    middle = left.astype(BF16)
    low = (left - middle.astype(F32)).astype(BF16)
    parts = jnp.concatenate(
        [high.astype(F32), middle.astype(F32), low.astype(F32), jnp.zeros((119, POINTS), F32)],
        axis=0,
    ).astype(BF16)
    order = jnp.broadcast_to(order_ref[...], (STEP, POINTS))
    slot = lax.broadcasted_iota(jnp.int32, (STEP, POINTS), 0)
    for first in range(0, POINTS, CHUNK):
        for row in range(first, first + CHUNK, STEP):
            onehot[row : row + STEP, :] = jnp.where(order == slot + row, 1.0, 0.0).astype(BF16)
        placed = lax.dot_general(
            onehot[first : first + CHUNK, :], parts, LAST, preferred_element_type=F32
        )
        column_ref[first : first + CHUNK, 0:3] = placed[:, 0:3] + placed[:, 3:6] + placed[:, 6:9]
        message_ref[COLS : COLS + 16, first : first + CHUNK] = placed.T[0:16, :].astype(BF16)
    loads[2].wait()
    message_ref[0:COLS, :] = (obs_ref[...] / centre).astype(BF16)


def half_of_chip(block):
    wide = jnp.concatenate([block, block], axis=1)
    lane = lax.broadcasted_iota(jnp.int32, (COLS, 2 * RANK), 1)
    core = lax.rem(lax.axis_index("leaf"), 2)
    return jnp.where(lane // RANK == core, wide, 0.0).astype(BF16)


def basis_kernel(message_ref, proxy_ref, basis_ref, wide_ref):
    rows = coordinate_rows(message_ref[COLS : COLS + 16, :])
    squared = None
    for c in range(3):
        apart = proxy_ref[:, c : c + 1] * SCALE - rows[c : c + 1, :]
        squared = apart * apart if squared is None else squared + apart * apart
    basis = distance_kernel(squared).astype(BF16)
    basis_ref[...] = basis
    wide_ref[:, 0:POINTS] = message_ref[...]
    wide_ref[0:COLS, POINTS:] = half_of_chip(
        lax.dot_general(message_ref[0:COLS, :], basis, LAST, preferred_element_type=F32)
    )
    wide_ref[COLS : COLS + 16, POINTS:] = jnp.zeros((16, 2 * RANK), BF16)


def fill_column(column_ref, filled):
    for c in range(3):
        for row in range(0, POINTS, CHUNK):
            filled[c, row : row + CHUNK, :] = jnp.broadcast_to(
                column_ref[row : row + CHUNK, c : c + 1], (CHUNK, 128)
            )


def build_and_apply(block, column_ref, tile_ref, total_ref, first_block):
    coords = coordinate_rows(block[COLS : COLS + 16, 0:POINTS])
    rows = [jnp.broadcast_to(coords[c : c + 1, :], (STEP, POINTS)) for c in range(3)]
    field = block[0:COLS, 0:POINTS]
    for first in range(0, POINTS, CHUNK):
        for row in range(first, first + CHUNK, STEP):
            pieces = []
            for lane in range(0, POINTS, 128):
                squared = None
                for c in range(3):
                    apart = column_ref[c, row : row + STEP, :] - rows[c][:, lane : lane + 128]
                    squared = apart * apart if squared is None else squared + apart * apart
                pieces.append(distance_kernel(squared).astype(BF16))
            tile_ref[row : row + STEP, :] = jnp.concatenate(pieces, axis=1)
        product = lax.dot_general(
            tile_ref[first : first + CHUNK, :], field, LAST, preferred_element_type=F32
        )
        if first_block:
            total_ref[first : first + CHUNK, :] = product
        else:
            total_ref[first : first + CHUNK, :] += product


def own_tile_kernel(own_ref, column_ref, own_tile, total_ref, filled):
    fill_column(column_ref, filled)
    build_and_apply(own_ref, filled, own_tile, total_ref, True)


def partner_tile_kernel(flag_ref, partner_ref, column_ref, total_in, tile_ref, total_ref, filled):
    total_ref[...] = total_in[...]

    @pl.when(flag_ref[0] != 0)
    def _():
        fill_column(column_ref, filled)
        build_and_apply(partner_ref, filled, tile_ref, total_ref, False)


def pair_tiles_kernel(place, flag_ref, *refs):
    *refs, filled = refs
    count = (len(refs) - 3) // 2
    column_ref, total_in, total_ref = refs[count], refs[count + 1], refs[-1]
    total_ref[...] = total_in[...]
    fill_column(column_ref, filled)
    for which in range(count):
        pair_ref, tiles_ref = refs[which], refs[count + 2 + which]

        @pl.loop(0, 2)
        def _(at, which=which, pair_ref=pair_ref, tiles_ref=tiles_ref):
            @pl.when(flag_ref[place + 2 * which + at] != 0)
            def _():
                build_and_apply(pair_ref.at[at], filled, tiles_ref.at[at], total_ref, False)


def apply_own_kernel(wide_ref, tile_ref, total_ref):
    total_ref[...] = lax.dot_general(
        tile_ref[...], wide_ref[:, 0:POINTS], LAST, preferred_element_type=F32
    )


def apply_near_kernel(places, flag_ref, *refs):
    count = len(places)
    total_ref = refs[-1]
    total_ref[...] = refs[-2][...]
    for which, (place, blocks) in enumerate(places):
        for at in range(blocks):

            @pl.when(flag_ref[place + at] != 0)
            def _(which=which, at=at, blocks=blocks):
                block, tile = refs[which], refs[count + which]
                if blocks == 2:
                    block, tile = block.at[at], tile.at[at]
                total_ref[...] += lax.dot_general(
                    tile[...], block[0:COLS, 0:POINTS], LAST, preferred_element_type=F32
                )


def select_kernel(*refs):
    gathered, wanted, within_ref = refs[0:2], refs[2], refs[3]
    sends, inside_ref, held = refs[4:8], refs[8], refs[9]
    held[0:8] = gathered[0][...]
    held[8:16] = gathered[1][...]
    mine = lax.axis_index("leaf")
    my_y, my_x, my_core = mine // 8, lax.rem(mine // 2, 4), lax.rem(mine, 2)
    low_half = lax.broadcasted_iota(jnp.int32, (COLS, 2 * RANK), 1) < RANK

    def pair(first, second):
        halves = []
        for leaf, half in ((first, 0), (second, 1)):
            y, x, core = leaf // 8, lax.rem(leaf // 2, 4), lax.rem(leaf, 2)
            dx, dy = x ^ my_x, y ^ my_y
            at = (dx ^ (dx // 2)) * 4 + (dy ^ (dy // 2))
            block = held[at].astype(F32)
            turned = jnp.concatenate([block[:, RANK:], block[:, :RANK]], axis=1)
            same = jnp.full((COLS, 2 * RANK), core, jnp.int32) == half
            halves.append(jnp.where(same, block, turned))
        return jnp.where(low_half, halves[0], halves[1]).astype(BF16)

    for j in (1, 2, 3, 4):
        k = jnp.where(my_core == 0, j - 1, 7 - j)
        for who in range(1 if j == 4 else 2):
            at = (2 * (j - 1) + who) * 14 + 2 * k
            sends[j - 1][who] = pair(wanted[at], wanted[at + 1])
    for k in range(3):
        inside_ref[k] = pair(within_ref[0, 2 * k], within_ref[0, 2 * k + 1])


def kernel_part(inside_ref, arrived, passed_ref, coupling_ref, basis_ref, total_ref):
    core = lax.rem(lax.axis_index("leaf"), 2)
    spread = None

    def add(spread, source, first):
        for a in range(2):
            half = source.astype(F32)[:, a * RANK : a * RANK + RANK].astype(BF16)
            term = lax.dot_general(half, coupling_ref[0, first + a], LAST, preferred_element_type=F32)
            spread = term if spread is None else spread + term
        return spread

    for k in range(3):
        spread = add(spread, inside_ref[k], 2 * k)
    for j in (1, 2, 3):
        near, away = 6 + 2 * (j - 1), 6 + 2 * (7 - j)
        spread = add(spread, arrived[j - 1][0], jnp.where(core == 0, near, away))
        spread = add(spread, passed_ref[j - 1], jnp.where(core == 0, away, near))
    spread = add(spread, arrived[3][0], 6 + 2 * 3)
    far = jnp.dot(spread.astype(BF16), basis_ref[...], preferred_element_type=F32)
    return (total_ref[...].T + far) / kernel_scale


def update_kernel(*refs):
    obs_ref, noise_ref, inside_ref, arrived, passed_ref = refs[0], refs[1], refs[2], refs[3:7], refs[7]
    coupling_ref, basis_ref, total_ref = refs[8:11]
    gain_ref, residual_ref, direction_ref, wide_ref = refs[11:15]
    right_side = obs_ref[...]
    direction = right_side / centre
    applied = noise_ref[...] * direction + kernel_part(
        inside_ref, arrived, passed_ref, coupling_ref, basis_ref, total_ref
    )
    residual = right_side - applied
    later = ALONG * direction + ACROSS * residual
    rounded = later.astype(BF16)
    wide_ref[:, 0:POINTS] = rounded
    wide_ref[:, POINTS:] = half_of_chip(
        lax.dot_general(rounded, basis_ref[...], LAST, preferred_element_type=F32)
    )
    gain_ref[...] = direction + later
    residual_ref[...] = residual
    direction_ref[...] = later


def finish_kernel(*refs):
    before_ref, direction_ref, noise_ref, inside_ref, arrived, passed_ref = (*refs[0:4], refs[4:8], refs[8])
    coupling_ref, basis_ref, total_ref = refs[9:12]
    applied = noise_ref[...] * direction_ref[...] + kernel_part(
        inside_ref, arrived, passed_ref, coupling_ref, basis_ref, total_ref
    )
    refs[12][...] = before_ref[...] - applied


def from_ahead(value, axis, steps):
    count = lax.axis_size(axis)
    return lax.ppermute(value, axis, [(s, (s - steps) % count) for s in range(count)])


def exchange(value, axis, distance):
    count = lax.axis_size(axis)
    return lax.ppermute(value, axis, [(s, s ^ distance) for s in range(count)])


def from_both_sides(value, axis, chips, per_chip):
    count = lax.axis_size(axis)
    pairs = []
    for s in range(count):
        steps = -chips * per_chip if s % 2 == 0 else chips * per_chip
        pairs.append((s, (s + steps) % count))
    return lax.ppermute(value, axis, pairs)


def from_partner(value):
    return exchange(value, "leaf", 1)


def after(value, *others):
    return lax.optimization_barrier((value, *others))[0]


def pick(halves, wanted, far_within):
    one, two = shape((1, COLS, 2 * RANK), BF16), shape((2, COLS, 2 * RANK), BF16)
    return call(
        select_kernel,
        [two, two, two, one, shape((3, COLS, 2 * RANK), BF16)],
        [VMEM] * 2 + [SMEM] * 2,
        (*halves, wanted, far_within),
        0.7,
        [pltpu.VMEM((16, COLS, 2 * RANK), BF16)],
        name="select",
    )


def exchanges(wide, steps, wanted, far_within, after):
    partner = from_partner(wide)
    total = steps[0]()
    partner = after(partner, total)
    chip = (wide[:COLS, POINTS:] + partner[:COLS, POINTS:])[None]
    rows = exchange(chip, "leaf", 8)
    total = steps[1](partner, total)
    rows = after(rows, total)
    two = jnp.concatenate([chip, rows])
    rows = exchange(two, "leaf", 24)
    pair = after(jnp.stack([wide[:, :POINTS], partner[:, :POINTS]]), two)
    first = from_both_sides(pair, BOTH, 1, 2)
    four = jnp.concatenate([two, rows])
    columns = exchange(four, "leaf", 2)
    first = after(first, four)
    second = from_both_sides(first, BOTH, 1, 2)
    passed_first = from_partner(first)
    total = steps[2](first, total)
    columns = after(columns, total)
    eight = jnp.concatenate([four, columns])
    columns = exchange(eight, "leaf", 6)
    passed_second = from_partner(second)
    total = steps[3](passed_first, total)
    columns = after(columns, total)
    *sends, inside = pick((eight, columns), wanted, far_within)
    arrived = [from_both_sides(sends[j - 1], BOTH, j, 32) for j in (1, 2, 3, 4)]
    total = steps[4](second, passed_second, total)
    arrived = [after(a, total) for a in arrived]
    passed = from_partner(after(jnp.stack([arrived[j][1] for j in range(3)]), arrived[3]))
    return (inside, *arrived, passed), total


def local(
    observations,
    coordinates,
    proxies,
    noise_variance,
    ordering,
    near_list,
    far_within,
    far_across,
    couplings,
):
    leaves = lax.axis_size(BOTH)
    leaf_id = lax.axis_index(BOTH)
    core = leaf_id % 2
    listed = jnp.concatenate([far_across, from_partner(far_across)])
    asked = jnp.stack([from_both_sides(listed, BOTH, -j, 32) for j in (1, 2, 3, 4)]).reshape(112)
    offsets = jnp.array([1, 2, 3, -1, -2, 4, 5, -3, -4], jnp.int32) * (1 - 2 * core)
    targets = (leaf_id + offsets + leaves) % leaves
    flags = jnp.any(near_list[0][None, :] == targets[:, None], axis=1).astype(jnp.int32)
    noise = noise_variance[None, :]

    message, column = call(
        prepare_kernel,
        [shape((COLS + 16, POINTS), BF16), shape((POINTS, 128), F32)],
        [pl.BlockSpec(memory_space=pltpu.HBM)] * 3,
        (observations, ordering, coordinates),
        2.0,
        [
            pltpu.VMEM((POINTS, POINTS), BF16),
            pltpu.VMEM((COLS, POINTS), F32),
            pltpu.VMEM((1, POINTS), jnp.int32),
            pltpu.VMEM((3, POINTS), F32),
            pltpu.SemaphoreType.DMA((3,)),
        ],
        name="prepare",
    )
    basis, wide = call(
        basis_kernel,
        [shape((RANK, POINTS), BF16), shape((COLS + 16, POINTS + 2 * RANK), BF16)],
        [VMEM] * 2,
        (message, proxies[0].T),
        0.7,
        name="basis",
    )
    tile_shape, total_shape = shape((POINTS, POINTS), BF16), shape((POINTS, COLS), F32)
    tiles, filled = [], [pltpu.VMEM((3, POINTS, 128), F32)]

    def build_own():
        tile, total = call(
            own_tile_kernel, [tile_shape, total_shape], [VMEM] * 2, (wide, column), 2.0, filled, name="own_tile"
        )
        tiles.append(tile)
        return total

    def build_partner(partner, total):
        tile, total = call(
            partner_tile_kernel,
            [tile_shape, total_shape],
            [SMEM] + [VMEM] * 3,
            (flags, partner, column, total),
            2.0,
            filled,
            name="partner_tile",
        )
        tiles.append(tile)
        return total

    def build_pairs(place, *pairs_total):
        *pairs, total = pairs_total
        *built, total = call(
            functools.partial(pair_tiles_kernel, place),
            [shape((2, POINTS, POINTS), BF16)] * len(pairs) + [total_shape],
            [SMEM] + [VMEM] * (len(pairs) + 2),
            (flags, *pairs, column, total),
            4.0 * len(pairs),
            filled,
            name="pair_tiles",
        )
        tiles.extend(built)
        return total

    far, total = exchanges(
        wide,
        [build_own, build_partner]
        + [functools.partial(build_pairs, place) for place in (1, 3, 5)],
        asked,
        far_within,
        after,
    )
    field = shape((COLS, POINTS), F32)
    gain, residual, direction, wide = call(
        update_kernel,
        [field, field, field, shape((COLS, POINTS + 2 * RANK), BF16)],
        [VMEM] * 11,
        (observations, noise, *far, couplings, basis, total),
        1.5,
        name="update",
    )

    def apply_own():
        return call(
            apply_own_kernel, total_shape, [VMEM] * 2, (wide, tiles[0]), 0.7, name="apply_own"
        )

    held = []

    def hold(block, total):
        held.append(block)
        return total

    def apply_near(places, *blocks_total):
        *blocks, total = blocks_total
        matching = [tiles[1 + (place + 1) // 2] for place, _ in places]
        return call(
            functools.partial(apply_near_kernel, places),
            total_shape,
            [SMEM] + [VMEM] * (2 * len(places) + 1),
            (flags, *blocks, *matching, total),
            0.7 * sum(count for _, count in places),
            name="apply_near",
        )

    far, total = exchanges(
        wide,
        [
            apply_own,
            hold,
            lambda first, total: apply_near(((0, 1), (1, 2)), held.pop(), first, total),
            hold,
            lambda *rest: apply_near(((3, 2), (5, 2), (7, 2)), held.pop(), *rest),
        ],
        asked,
        far_within,
        lambda value, *others: value,
    )
    residual = call(
        finish_kernel,
        field,
        [VMEM] * 12,
        (residual, direction, noise, *far, couplings, basis, total),
        1.0,
        name="finish",
    )
    return (gain, residual)


def solution(mesh):
    placed = (
        P(None, ("group", "leaf")),
        P(None, ("group", "leaf")),
        P(("group", "leaf"), None, None),
        P(("group", "leaf")),
        P(("group", "leaf"), None),
        P(("group", "leaf"), None),
        P(("group", "leaf"), None),
        P(("group", "leaf"), None, None),
        P(("group", "leaf"), None, None, None),
    )
    return jax.shard_map(
        local,
        mesh=mesh,
        in_specs=placed,
        out_specs=(P(None, ("group", "leaf")), P(None, ("group", "leaf"))),
        check_vma=False,
    )
```
